32 devices in a mesh: facet: 8 (over z, x), freq: 4 (over y, core).
Axes of the slice: x: 2, y: 2, z: 4, core: 2. Of those that a mesh axis runs over, the one named last changes fastest.
Arguments:
- visibilities: float32 [8, 10, 2, 128, 128], P('facet', None, None, 'freq'), may hold values from -6 to 6
- coords: float32 [8, 10, 3, 128], P('facet'), may hold values from -1500 to 1500, as said below
- corners: int32 [2, 8, 10], replicated, may hold values from 0 to 480
- owners: int32 [2], replicated, may hold values from 0 to 7, as said below
- assign: int32 [8, 20], P('facet'), may hold values from 0 to 19, as said below
- counts: int32 [8], P('facet'), may hold values from 2 to 20, as said below
Outputs:
- dirty: float32 [8, 512, 512], P('facet', 'freq')
The draws below stay inside these ranges and needn't reach their ends.
Inputs may be any that keep to these rules, and one draw needn't show every extreme that they name: `owners`: the two sets lie in different slots, one of them in the last slot. `assign`: each facet's row is a permutation of the 20 block numbers; only its first counts entries are gridded. `counts`: some facet grids all 20 blocks. `coords`: at every channel, u and v of each row of a block lie within 12 cells of the centre of that block's subgrid.
All inputs are finite; a program needn't handle non-finite values.
Results may differ from the reference program's by a relative error of at most 0.0037.
Values sent between devices are 32-bit elements; how exact they have to be, the bound alone decides.
No kernel may reach another device: no remote copies, remote signals or barrier semaphores. Data moves between devices by JAX's collectives and lax.ppermute only.
A program may use at most 64 MiB of HBM per device.

```python
import math
import jax
import jax.numpy as jnp
from jax import lax

SUB = 32
G = 512
BLK = 128
CH = 32
BPC = 10
SMAX = 20
CHANS = 128
N_FACET = 8
N_FREQ = 4


def corner_table(key):
    return jax.random.randint(jax.random.fold_in(key, 11), (2, N_FACET, BPC), 0, G - SUB + 1).astype(jnp.int32)


def draw_corners(key, part):
    return corner_table(key)


def draw_coords(key, part):
    corner_cells = corner_table(key).astype(jnp.float32)
    centre_cells = jnp.transpose(corner_cells, (1, 2, 0))[:, :, :, None] + (SUB // 2 - G // 2)
    offsets = jax.random.uniform(jax.random.fold_in(key, 21), (N_FACET, BPC, 2, BLK), minval=-8.0, maxval=8.0)
    depth = jnp.clip(300.0 * jax.random.normal(jax.random.fold_in(key, 22), (N_FACET, BPC, 1, BLK)), -1500.0, 1500.0)
    planar = (centre_cells + offsets) / 1.01
    return jnp.concatenate([planar, depth], axis=2).astype(jnp.float32)


def draw_owners(key, part):
    other_slot = jax.random.randint(jax.random.fold_in(key, 13), (), 0, N_FACET - 1)
    last_slot = jnp.full((), N_FACET - 1, jnp.int32)
    flip = jax.random.randint(jax.random.fold_in(key, 17), (), 0, 2)
    first = jnp.where(flip == 1, last_slot, other_slot)
    second = jnp.where(flip == 1, other_slot, last_slot)
    return jnp.stack([first, second]).astype(jnp.int32)


def draw_assign(key, part):
    scores = jax.random.randint(jax.random.fold_in(key, 14), (N_FACET, SMAX), 0, 1048576) * SMAX
    scores = scores + jnp.arange(SMAX, dtype=jnp.int32)[None, :]
    return jnp.argsort(scores, axis=1, stable=True).astype(jnp.int32)


def draw_counts(key, part):
    divisor = jax.random.randint(jax.random.fold_in(key, 15), (N_FACET,), 1, 9)
    chosen = jax.random.randint(jax.random.fold_in(key, 16), (), 0, N_FACET)
    return jnp.where(jnp.arange(N_FACET) == chosen, SMAX, SMAX // divisor).astype(jnp.int32)


def level_of(stream_key, shape, shards, least, high):
    level = 1.0
    for dim, blocks in shards:
        steps = jax.random.uniform(jax.random.fold_in(jax.random.fold_in(stream_key, 6), dim), (blocks,), jnp.float32, least / len(shards), high / len(shards))
        level = level * jnp.repeat(jnp.exp(steps), shape[dim] // blocks).reshape((-1,) + (1,) * (len(shape) - 1 - dim))
    return level


def gaussian(stream_key, dims, deviation, limit, cuts=(), kind=jnp.bfloat16):
    array = jax.random.normal(stream_key, dims, jnp.float32) * deviation
    if len(cuts) > 0:
        array = level_of(stream_key, dims, cuts, -0.22, 0.18) * array
    return jnp.clip(array, min=-limit, max=limit).astype(kind)


def setup_inputs(seed: int = 0) -> dict:
    key_list = jax.random.split(jax.random.key(seed), 7)
    visibilities = gaussian(key_list[0], (N_FACET, BPC, 2, CHANS, BLK), 1.0, 6.0, ((0, 8), (3, 4)), jnp.float32)
    coords = draw_coords(jax.random.fold_in(key_list[6], 71), 0)
    corners = draw_corners(jax.random.fold_in(key_list[6], 71), 0)
    owners = draw_owners(jax.random.fold_in(key_list[6], 71), 0)
    assign = draw_assign(jax.random.fold_in(key_list[6], 71), 0)
    counts = draw_counts(jax.random.fold_in(key_list[6], 71), 0)
    return {"visibilities": visibilities, "coords": coords, "corners": corners, "owners": owners, "assign": assign, "counts": counts}


two_pi = 2.0 * math.pi
field_width = 0.02
band_spread = 0.02
batch_items = 8
highest = lax.Precision.HIGHEST

def facet_center(facet_id, facet_total):
    row_total = facet_total // 8
    column = (facet_id % 8).astype(jnp.float32) - 3.5
    row_pos = (facet_id // 8).astype(jnp.float32) - (row_total - 1) / 2.0
    radius = field_width * field_width * (column * column + row_pos * row_pos)
    w_shift = -radius / (1.0 + jnp.sqrt(1.0 - radius))
    return (column, row_pos, w_shift)

def subgrid_tables():
    offsets = jnp.arange(SUB, dtype=jnp.int32) - SUB // 2
    position = offsets.astype(jnp.float32)
    profile = 1.0 - 0.8 * (position / (SUB / 2.0)) ** 2
    taper_square = profile[:, None] * profile[None, :]
    phase_index = offsets[:, None] * offsets[None, :] % SUB
    phase_angle = -two_pi * phase_index.astype(jnp.float32) / SUB
    return (position, taper_square, jnp.cos(phase_angle), jnp.sin(phase_angle))

def image_tables():
    offsets = jnp.arange(G, dtype=jnp.int32) - G // 2
    phase_index = offsets[:, None] * offsets[None, :] % G
    phase_angle = two_pi * phase_index.astype(jnp.float32) / G
    return (jnp.cos(phase_angle), jnp.sin(phase_angle))

def subgrid_terms(vis_blocks, coord_blocks, freq_ratio, corner_u, corner_v, column, row_pos, w_shift, tables):
    position = tables[0]
    item_total = vis_blocks.shape[0]
    scaled = coord_blocks[:, :, None, :] * freq_ratio[None, None, :, None]
    u_cells = scaled[:, 0]
    v_cells = scaled[:, 1]
    w_waves = scaled[:, 2]
    rotation = two_pi * (u_cells * column[:, None, None] + v_cells * row_pos[:, None, None] + w_waves * w_shift[:, None, None])
    rot_real = jnp.cos(rotation)
    rot_imag = jnp.sin(rotation)
    vis_real = vis_blocks[:, 0] * rot_real - vis_blocks[:, 1] * rot_imag
    vis_imag = vis_blocks[:, 0] * rot_imag + vis_blocks[:, 1] * rot_real
    centre_shift = G // 2 - SUB // 2
    delta_u = (u_cells + (centre_shift - corner_u).astype(jnp.float32)[:, None, None]).reshape(item_total, 1, -1)
    delta_v = (v_cells + (centre_shift - corner_v).astype(jnp.float32)[:, None, None]).reshape(item_total, 1, -1)
    angle_u = two_pi / SUB * delta_u * position[None, :, None]
    left_factor = jnp.concatenate([jnp.cos(angle_u), jnp.sin(angle_u)], axis=2).astype(jnp.bfloat16)
    angle_v = two_pi / SUB * delta_v * position[None, :, None]
    wave_real = jnp.cos(angle_v)
    wave_imag = jnp.sin(angle_v)
    flat_real = vis_real.reshape(item_total, 1, -1)
    flat_imag = vis_imag.reshape(item_total, 1, -1)
    right_real = flat_real * wave_real - flat_imag * wave_imag
    right_imag = flat_real * wave_imag + flat_imag * wave_real
    upper_rows = jnp.concatenate([right_real, -right_imag], axis=2)
    lower_rows = jnp.concatenate([right_imag, right_real], axis=2)
    right_factor = jnp.concatenate([upper_rows, lower_rows], axis=1).astype(jnp.bfloat16)
    return (left_factor, right_factor)

def subgrid_finish(product, tables):
    taper_square, dft_real, dft_imag = (tables[1], tables[2], tables[3])
    image_real = product[:, :, :SUB] * taper_square
    image_imag = product[:, :, SUB:] * taper_square
    half_real = jnp.einsum('pl,slm->spm', dft_real, image_real, precision=highest) - jnp.einsum('pl,slm->spm', dft_imag, image_imag, precision=highest)
    half_imag = jnp.einsum('pl,slm->spm', dft_real, image_imag, precision=highest) + jnp.einsum('pl,slm->spm', dft_imag, image_real, precision=highest)
    uv_real = jnp.einsum('spm,qm->spq', half_real, dft_real, precision=highest) - jnp.einsum('spm,qm->spq', half_imag, dft_imag, precision=highest)
    uv_imag = jnp.einsum('spm,qm->spq', half_real, dft_imag, precision=highest) + jnp.einsum('spm,qm->spq', half_imag, dft_real, precision=highest)
    return jnp.stack([uv_real, uv_imag], axis=1)

def add_pieces(uv_grid, pieces, corner_u, corner_v, weights):
    zero_index = jnp.zeros((), jnp.int32)
    for item in range(batch_items):
        anchor = (zero_index, corner_u[item].astype(jnp.int32), corner_v[item].astype(jnp.int32))
        current = lax.dynamic_slice(uv_grid, anchor, (2, SUB, SUB))
        uv_grid = lax.dynamic_update_slice(uv_grid, current + pieces[item] * weights[item], anchor)
    return uv_grid

def reference(visibilities, coords, corners, owners, assign, counts):
    tables = subgrid_tables()
    channel_total = CH * N_FREQ
    freq_ratio = 1.0 + band_spread * jnp.arange(channel_total, dtype=jnp.float32) / channel_total
    vis_all = visibilities[owners].reshape(2 * BPC, 2, channel_total, BLK)
    coord_all = coords[owners].reshape(2 * BPC, 3, BLK)
    corner_all = corners[:, owners, :].reshape(2, 2 * BPC)
    cos_table, sin_table = image_tables()
    image_scale = 1.0 / (SUB * SUB * math.sqrt(SMAX * BLK * channel_total))

    def one_facet(facet_id):
        column, row_pos, w_shift = facet_center(facet_id, N_FACET)
        item_count = counts[facet_id]
        block_list = assign[facet_id]

        def grid_step(batch_index, uv_grid):
            item_index = batch_index * batch_items + jnp.arange(batch_items, dtype=jnp.int32)
            weights = (item_index < item_count).astype(jnp.float32)
            block_index = jnp.take(block_list, jnp.minimum(item_index, SMAX - 1))
            corner_u = jnp.take(corner_all[0], block_index)
            corner_v = jnp.take(corner_all[1], block_index)
            left_factor, right_factor = subgrid_terms(jnp.take(vis_all, block_index, axis=0), jnp.take(coord_all, block_index, axis=0), freq_ratio, corner_u, corner_v, jnp.full((batch_items,), column), jnp.full((batch_items,), row_pos), jnp.full((batch_items,), w_shift), tables)
            product = jnp.einsum('slk,smk->slm', left_factor.astype(jnp.float32), right_factor.astype(jnp.float32), precision=highest)
            pieces = subgrid_finish(product, tables)
            return add_pieces(uv_grid, pieces, corner_u, corner_v, weights)
        batch_total = (item_count + batch_items - 1) // batch_items
        uv_grid = lax.fori_loop(0, batch_total, grid_step, jnp.zeros((2, G, G), jnp.float32))
        half_real = jnp.dot(cos_table, uv_grid[0], precision=highest, preferred_element_type=jnp.float32) - jnp.dot(sin_table, uv_grid[1], precision=highest, preferred_element_type=jnp.float32)
        half_imag = jnp.dot(cos_table, uv_grid[1], precision=highest, preferred_element_type=jnp.float32) + jnp.dot(sin_table, uv_grid[0], precision=highest, preferred_element_type=jnp.float32)
        image_part = jnp.dot(half_real, cos_table, precision=highest, preferred_element_type=jnp.float32) - jnp.dot(half_imag, sin_table, precision=highest, preferred_element_type=jnp.float32)
        return image_part * image_scale
    return lax.map(one_facet, jnp.arange(N_FACET, dtype=jnp.int32))
```

```python
import math

import jax
import jax.numpy as jnp
import numpy as np
from jax import lax
from jax.experimental import pallas as pl
from jax.experimental.pallas import tpu as pltpu
from jax.sharding import PartitionSpec as P

SUB = 32
G = 512
HALF = SUB // 2
COLUMNS = 8

two_pi = 2.0 * math.pi
field_width = 0.02
band_spread = 0.02
centre_shift = G // 2 - SUB // 2

SIN_POLY = (6.2831853, -41.34170041, 81.6051314, -76.70301553, 42.02592778, -14.89984801, 3.23813768)
COS_POLY = (0.99999999, -19.7392045, 64.9391175, -85.45013994, 60.16763282, -25.96760244, 6.52865863)


def poly(square, coefficients):
    total = jnp.full_like(square, coefficients[-1])
    for coefficient in coefficients[-2::-1]:
        total = total * square + coefficient
    return total


def cos_sin(turns):
    rest = turns - jnp.round(turns)
    square = rest * rest
    return poly(square, COS_POLY), rest * poly(square, SIN_POLY)


def times(a, b):
    return a[0] * b[0] - a[1] * b[1], a[0] * b[1] + a[1] * b[0]


def swap_low(value):
    return (value & ~3) | ((value & 1) << 1) | ((value >> 1) & 1)


def grid_kernel(
    owners_ref, corners_ref, coords_ref, vis_ref, keep_ref, send_ref, z_ref, base_ref, step_ref, left_ref, right_ref
):
    me = lax.axis_index("facet")
    band = lax.axis_index("freq")
    band_total = lax.axis_size("freq")
    facet_rows = lax.axis_size("facet") // COLUMNS
    core = band & 1
    facet_row = pl.program_id(0)
    block = pl.program_id(1)
    channels, lanes = vis_ref.shape[3], vis_ref.shape[4]
    half_blocks = pl.num_programs(1) // 2

    @pl.when(jnp.logical_or(owners_ref[0] == me, owners_ref[1] == me))
    def _():
        corner_u = corners_ref[0, me, block]
        corner_v = corners_ref[1, me, block]
        channel = (band * channels + lax.broadcasted_iota(jnp.int32, (channels, lanes), 0)).astype(jnp.float32)
        ratio = 1.0 + band_spread * channel / (channels * band_total)
        u_cells = coords_ref[0, 0, 0:1, :] * ratio
        v_cells = coords_ref[0, 0, 1:2, :] * ratio
        w_waves = coords_ref[0, 0, 2:3, :] * ratio
        shift_u = centre_shift - corner_u
        delta_u = u_cells + shift_u.astype(jnp.float32)
        delta_v = v_cells + (centre_shift - corner_v).astype(jnp.float32)
        row_pos = facet_row.astype(jnp.float32) - (facet_rows - 1) / 2.0
        row_vec = jnp.full((8, lanes), row_pos, jnp.float32)
        common = (
            v_cells * row_pos - (delta_u + delta_v) * (0.5 / SUB) + 0.5 * (shift_u & 1).astype(jnp.float32)
        )
        vis = (vis_ref[0, 0, 0], vis_ref[0, 0, 1])
        for g in range(COLUMNS // 2):
            radius = field_width * field_width * ((g + 0.5) ** 2 + row_vec * row_vec)
            w_shift = (-radius / (1.0 + jnp.sqrt(1.0 - radius)))[0:1]
            turned = times(vis, cos_sin(common + w_waves * w_shift))
            z_ref[2 * g] = turned[0]
            z_ref[2 * g + 1] = turned[1]
        for axis, delta in enumerate((delta_u, delta_v)):
            wave = cos_sin(delta * (0.5 / SUB))
            step = times(wave, wave)
            for j in range(8):
                base_ref[2 * axis, pl.ds(j, channels, stride=8), :] = wave[0]
                base_ref[2 * axis + 1, pl.ds(j, channels, stride=8), :] = wave[1]
                if j < 7:
                    wave = times(wave, step)
            for _ in range(3):
                step = times(step, step)
            step_ref[2 * axis] = step[0]
            step_ref[2 * axis + 1] = step[1]

        chunk = channels // 4
        product = None
        for first in range(0, channels, chunk):
            for c in range(first, first + chunk):
                at = slice(c * lanes, (c + 1) * lanes)
                step = (step_ref[0, c : c + 1, :], step_ref[1, c : c + 1, :])
                twice = 2.0 * step[0]
                wave = (base_ref[0, 8 * c : 8 * c + 8, :], base_ref[1, 8 * c : 8 * c + 8, :])
                after = times(wave, step)
                for i in range(COLUMNS):
                    for part in range(2):
                        left_ref[128 * part + 16 * i : 128 * part + 16 * i + 16, at] = jnp.concatenate(
                            [wave[part], after[part]], axis=0
                        ).astype(jnp.bfloat16)
                    if i < COLUMNS - 1:
                        wave = tuple(twice * after[part] - wave[part] for part in range(2))
                        after = tuple(twice * wave[part] - after[part] for part in range(2))
                step = (step_ref[2, c : c + 1, :], step_ref[3, c : c + 1, :])
                wave = (base_ref[2, 8 * c : 8 * c + 8, :], base_ref[3, 8 * c : 8 * c + 8, :])
                after = times(wave, step)
                both = tuple(jnp.concatenate([wave[part], after[part]], axis=0) for part in range(2))
                for g in range(COLUMNS // 2):
                    for part in range(2):
                        turned = z_ref[2 * g + part, c : c + 1, :]
                        for kind in range(2):
                            row = 64 * g + 32 * part + 16 * kind
                            right_ref[row : row + 16, at] = (turned * both[kind]).astype(jnp.bfloat16)
            at = slice(first * lanes, (first + chunk) * lanes)
            term = lax.dot_general(
                right_ref[:, at],
                left_ref[:, at],
                (((1,), (1,)), ((), ())),
                preferred_element_type=jnp.float32,
            )
            product = term if product is None else product + term

        group = lax.broadcasted_iota(jnp.int32, (HALF, 128), 1) // SUB
        half = block // half_blocks
        row = pl.multiple_of((block - half * half_blocks) * HALF, HALF)
        for sign in (1, -1):
            for g in range(COLUMNS // 2):
                part = [product[64 * g + 16 * k : 64 * g + 16 * k + 16] for k in range(4)]
                (rcc, rcs), (rsc, rss), (icc, ics), (isc, iss) = [(x[:, :128], x[:, 128:]) for x in part]
                kinds = (rcc - sign * ics, -(sign * rss + isc), icc + sign * rcs, rsc - sign * iss)
                tile = None
                for t in range(4):
                    moved = kinds[t] if t == g else pltpu.roll(kinds[t], SUB * ((t - g) % 4), 1)
                    tile = moved if tile is None else jnp.where(group == t, moved, tile)
                facet = facet_row * COLUMNS + (COLUMNS // 2 + g if sign == 1 else COLUMNS // 2 - 1 - g)
                straight = facet ^ me
                crossed = swap_low(straight)

                @pl.when(half == core)
                def _():
                    keep_ref[jnp.where(core == 1, crossed, straight), pl.ds(row, HALF), :] = tile

                @pl.when(half != core)
                def _():
                    send_ref[jnp.where(core == 0, crossed, straight), pl.ds(row, HALF), :] = tile


def grid_blocks(owners, corners, coords, visibilities):
    facet_total = lax.axis_size("facet")
    _, blocks, _, channels, lanes = visibilities.shape
    half_rows = blocks // 2 * HALF
    out = jax.ShapeDtypeStruct((facet_total, half_rows, 128), jnp.float32)
    return pl.pallas_call(
        grid_kernel,
        grid=(facet_total // COLUMNS, blocks),
        in_specs=[
            pl.BlockSpec(memory_space=pltpu.SMEM),
            pl.BlockSpec(memory_space=pltpu.SMEM),
            pl.BlockSpec((1, 1, 3, lanes), lambda r, b: (0, b, 0, 0)),
            pl.BlockSpec((1, 1, 2, channels, lanes), lambda r, b: (0, b, 0, 0, 0)),
        ],
        out_specs=[pl.BlockSpec(out.shape, lambda r, b: (0, 0, 0))] * 2,
        out_shape=[out, out],
        scratch_shapes=[
            pltpu.VMEM((COLUMNS, channels, lanes), jnp.float32),
            pltpu.VMEM((4, 8 * channels, lanes), jnp.float32),
            pltpu.VMEM((4, channels, lanes), jnp.float32),
            pltpu.VMEM((256, channels * lanes), jnp.bfloat16),
            pltpu.VMEM((256, channels * lanes), jnp.bfloat16),
        ],
        compiler_params=pltpu.CompilerParams(vmem_limit_bytes=48 * 1024 * 1024),
        name="grid_blocks",
    )(owners, corners, coords, visibilities)


def image_tables(band_total, scale):
    offsets = np.arange(SUB) - HALF
    pixels = np.arange(G) - G // 2
    taper = 1.0 - 0.8 * (offsets / HALF) ** 2
    spread = np.exp(2j * np.pi * np.outer(pixels, offsets) / G)
    table = spread @ np.exp(-2j * np.pi * np.outer(offsets, offsets) / SUB) * taper
    share = G // band_total
    first = np.zeros((2, band_total, 4, SUB, 4, share))
    for sign in range(2):
        for band in range(band_total):
            wave = table[band * share : (band + 1) * share, :: 1 if sign == 0 else -1].T
            for odd in range(2):
                first[sign, band, odd, :, 2 * odd] = wave.real
                first[sign, band, odd, :, 2 * odd + 1] = wave.imag
                first[sign, band, 2 + odd, :, 2 * odd] = -wave.imag
                first[sign, band, 2 + odd, :, 2 * odd + 1] = wave.real
    upper, lower = table.T[HALF:], table.T[HALF - 1 :: -1]
    second = np.stack([(upper + lower).real, (upper + lower).imag, (upper - lower).real, (upper - lower).imag]) * scale
    return first.reshape(2 * band_total, 4 * SUB, 4 * share).astype(np.float32), second.astype(np.float32)


def two_parts(value):
    high = value.astype(jnp.bfloat16)
    return high, (value - high.astype(jnp.float32)).astype(jnp.bfloat16)


def product_of(a, b, dims):
    def dot(x, y):
        return lax.dot_general(x, y, (dims, ((), ())), preferred_element_type=jnp.float32)

    return dot(a[0], b[0]) + (dot(a[0], b[1]) + dot(a[1], b[0]))


def image_kernel(
    table_ref, owners_ref, corners_ref, assign_ref, counts_ref, own_ref, other_ref, first_ref, second_ref, out_ref,
    turn_ref, weight_ref, left_ref, right_ref,
):
    band = lax.axis_index("freq")
    core = band & 1
    blocks = corners_ref.shape[2]
    share, pixels = out_ref.shape[1], out_ref.shape[2]
    half_rows = own_ref.shape[1]
    total = 2 * blocks

    for item in range(total):
        weight_ref[assign_ref[0, item]] = (item < counts_ref[0]).astype(jnp.int32)
    across = lax.broadcasted_iota(jnp.int32, (1, pixels), 1) - pixels // 2
    down = lax.broadcasted_iota(jnp.int32, (1, share), 1) - pixels // 2 + band * share
    for b in range(total):
        owner = owners_ref[b // blocks]
        turn_ref[b : b + 1, 0:pixels] = across * (corners_ref[1, owner, b % blocks] - centre_shift)
        turn_ref[b : b + 1, pixels : pixels + share] = down * (corners_ref[0, owner, b % blocks] - centre_shift)
    turns = (turn_ref[...] & (G - 1)).astype(jnp.float32) * (1.0 / G)
    turn_cos, turn_sin = cos_sin(turns)

    mine = core == 0
    pieces = []
    for s in range(2):
        own, other = own_ref[s], other_ref[s]
        pieces += [jnp.where(mine, own, other), jnp.where(mine, other, own)]
    subs = jnp.concatenate(pieces, axis=0)
    half = product_of(two_parts(subs), two_parts(first_ref[0]), ((1,), (0,)))
    second = [second_ref[k] for k in range(4)]
    for b in range(total):
        weight = weight_ref[b].astype(jnp.float32)
        c, s = turn_cos[b : b + 1, pixels:] * weight, turn_sin[b : b + 1, pixels:] * weight
        rows = half[HALF * b : HALF * b + HALF]
        for odd in range(2):
            real, imag = rows[:, 2 * odd * share : (2 * odd + 1) * share], rows[:, (2 * odd + 1) * share : (2 * odd + 2) * share]
            real, imag = times((real, imag), (c, s))
            for k, value in enumerate((real, imag)):
                at = 4 * HALF * b + (2 * odd + k) * HALF
                high, low = two_parts(value)
                left_ref[0, at : at + HALF] = high
                left_ref[1, at : at + HALF] = low
        c, s = turn_cos[b : b + 1, :pixels], turn_sin[b : b + 1, :pixels]
        for odd in range(2):
            real, imag = times((second[2 * odd], second[2 * odd + 1]), (c, s))
            for k, value in enumerate((real, -imag)):
                at = 4 * HALF * b + (2 * odd + k) * HALF
                high, low = two_parts(value)
                right_ref[0, at : at + HALF] = high
                right_ref[1, at : at + HALF] = low
    out_ref[0] = product_of((left_ref[0], left_ref[1]), (right_ref[0], right_ref[1]), ((0,), (0,)))


def image_blocks(owners, corners, assign, counts, own, other, channel_total, block_rows):
    facet_index, band_index = lax.axis_index("facet"), lax.axis_index("freq")
    band_total = lax.axis_size("freq")
    blocks = corners.shape[2]
    share = G // band_total
    scale = 1.0 / (SUB * SUB * math.sqrt(2 * blocks * block_rows * channel_total))
    first, second = image_tables(band_total, scale)
    left_half = (facet_index % COLUMNS < COLUMNS // 2).astype(jnp.int32)
    table = (left_half * band_total + band_index).reshape(1)
    rows = 2 * blocks * 4 * HALF
    smem = pl.BlockSpec(memory_space=pltpu.SMEM)
    return pl.pallas_call(
        image_kernel,
        grid_spec=pltpu.PrefetchScalarGridSpec(
            num_scalar_prefetch=1,
            grid=(1,),
            in_specs=[
                smem,
                smem,
                smem,
                smem,
                pl.BlockSpec(own.shape, lambda i, t: (0, 0, 0)),
                pl.BlockSpec(own.shape, lambda i, t: (0, 0, 0)),
                pl.BlockSpec((1,) + first.shape[1:], lambda i, t: (t[0], 0, 0)),
                pl.BlockSpec(second.shape, lambda i, t: (0, 0, 0)),
            ],
            out_specs=pl.BlockSpec((1, share, G), lambda i, t: (0, 0, 0)),
            scratch_shapes=[
                pltpu.VMEM((2 * blocks, G + share), jnp.int32),
                pltpu.SMEM((2 * blocks,), jnp.int32),
                pltpu.VMEM((2, rows, share), jnp.bfloat16),
                pltpu.VMEM((2, rows, G), jnp.bfloat16),
            ],
        ),
        out_shape=jax.ShapeDtypeStruct((1, share, G), jnp.float32),
        compiler_params=pltpu.CompilerParams(vmem_limit_bytes=48 * 1024 * 1024),
        name="image_blocks",
    )(table, owners, corners, assign, counts, own, other, jnp.asarray(first), jnp.asarray(second))


def swap(value, partner):
    facet_total, band_total = lax.axis_size("facet"), lax.axis_size("freq")
    pairs = []
    for f in range(facet_total):
        for q in range(band_total):
            to_f, to_q = partner(f, q)
            pairs.append((f * band_total + q, to_f * band_total + to_q))
    return lax.ppermute(value, ("facet", "freq"), pairs)


def on_device(visibilities, coords, corners, owners, assign, counts):
    facet_total, band_total = lax.axis_size("facet"), lax.axis_size("freq")
    facet_index, band_index = lax.axis_index("facet"), lax.axis_index("freq")
    channel_total = visibilities.shape[3] * band_total
    keep, send = grid_blocks(owners, corners, coords, visibilities)
    half_rows = keep.shape[1]
    held = (keep + swap(send, lambda f, q: (f, q ^ 1)))[None]
    for k in range(facet_total.bit_length() - 1):
        even, odd = (k, k ^ 1) if k < 2 else (k, k)
        parts = held.reshape(held.shape[0], -1, 2, half_rows, 128)
        kept, sent = parts[:, :, 0], parts[:, :, 1]
        came = swap(sent, lambda f, q: (f ^ (1 << (odd if q & 1 else even)), q))
        bit = jnp.where(band_index & 1 == 1, odd, even)
        other = ((owners ^ facet_index) >> bit & 1) == 1
        held = jnp.where(other[:, None, None, None], came, kept)
    held = held.reshape(2, half_rows, 128)
    for k in range(1, band_total.bit_length() - 1):
        held = held + swap(held, lambda f, q: (f, q ^ (1 << k)))
    other = swap(held, lambda f, q: (f, q ^ 1))
    return image_blocks(owners, corners, assign, counts, held, other, channel_total, visibilities.shape[4])


def solution(mesh):
    placed = (
        P("facet", None, None, "freq", None),
        P("facet", None, None, None),
        P(),
        P(),
        P("facet", None),
        P("facet"),
    )
    return jax.shard_map(
        on_device, mesh=mesh, in_specs=placed, out_specs=P("facet", "freq", None), check_vma=False
    )
```

```python
import math

import jax
import jax.numpy as jnp
import numpy as np
from jax import lax
from jax.experimental import pallas as pl
from jax.experimental.pallas import tpu as pltpu
from jax.sharding import PartitionSpec as P

SUB = 32
G = 512
HALF = SUB // 2
COLUMNS = 8
ROWS, BASE = 24, 40
PAD = 16

two_pi = 2.0 * math.pi
field_width = 0.02
band_spread = 0.02
centre_shift = G // 2 - SUB // 2

SIN_POLY = (6.2831853, -41.34170041, 81.6051314, -76.70301553, 42.02592778, -14.89984801, 3.23813768)
COS_POLY = (0.99999999, -19.7392045, 64.9391175, -85.45013994, 60.16763282, -25.96760244, 6.52865863)


def poly(square, coefficients):
    total = jnp.full_like(square, coefficients[-1])
    for coefficient in coefficients[-2::-1]:
        total = total * square + coefficient
    return total


def cos_sin(turns):
    rest = turns - jnp.round(turns)
    square = rest * rest
    return poly(square, COS_POLY), rest * poly(square, SIN_POLY)


def times(a, b):
    return a[0] * b[0] - a[1] * b[1], a[0] * b[1] + a[1] * b[0]


def swap_low(value):
    return (value & ~3) | ((value & 1) << 1) | ((value >> 1) & 1)


def grid_kernel(
    owners_hbm, corners_hbm, coords_hbm, vis_hbm, keep_ref, send_ref,
    owners_ref, corners_ref, coords_ref, vis_ref, small_sems, vis_sems, z_ref, base_ref, left_ref, right_ref,
):
    me = lax.axis_index("facet")
    band = lax.axis_index("freq")
    band_total = lax.axis_size("freq")
    facet_rows = lax.axis_size("facet") // COLUMNS
    core = band & 1
    facet_row = pl.program_id(0)
    block = pl.program_id(1)
    blocks = pl.num_programs(1)
    channels, lanes = vis_ref.shape[2], vis_ref.shape[3]
    half_blocks = blocks // 2

    small = [
        pltpu.make_async_copy(source, target, small_sems.at[k])
        for k, (source, target) in enumerate(
            ((owners_hbm, owners_ref), (corners_hbm, corners_ref), (coords_hbm, coords_ref))
        )
    ]
    large = [pltpu.make_async_copy(vis_hbm.at[0, b], vis_ref.at[b], vis_sems.at[b]) for b in range(vis_ref.shape[0])]

    @pl.when((facet_row == 0) & (block == 0))
    def _():
        for copy in small + large:
            copy.start()
        for copy in small:
            copy.wait()

    for b, copy in enumerate(large):

        @pl.when((facet_row == 0) & (block == b))
        def _():
            copy.wait()

    def build():
        corner_u = corners_ref[0, me, block]
        corner_v = corners_ref[1, me, block]
        channel = (band * channels + lax.broadcasted_iota(jnp.int32, (channels, lanes), 0)).astype(jnp.float32)
        ratio = 1.0 + band_spread * channel / (channels * band_total)
        u_cells = coords_ref[block, 0] * ratio
        v_cells = coords_ref[block, 1] * ratio
        w_waves = coords_ref[block, 2] * ratio
        shift_u = centre_shift - corner_u
        delta_u = u_cells + shift_u.astype(jnp.float32)
        delta_v = v_cells + (centre_shift - corner_v).astype(jnp.float32)
        row_pos = facet_row.astype(jnp.float32) - (facet_rows - 1) / 2.0
        row_vec = jnp.full((8, lanes), row_pos, jnp.float32)
        common = (
            v_cells * row_pos - (delta_u + delta_v) * (0.5 / SUB) + 0.5 * (shift_u & 1).astype(jnp.float32)
        )
        vis = (vis_ref[block, 0], vis_ref[block, 1])
        for g in range(COLUMNS // 2):
            radius = field_width * field_width * ((g + 0.5) ** 2 + row_vec * row_vec)
            w_shift = (-radius / (1.0 + jnp.sqrt(1.0 - radius)))[0:1]
            turned = times(vis, cos_sin(common + w_waves * w_shift))
            z_ref[pl.ds(2 * g, channels, stride=ROWS), :] = turned[0]
            z_ref[pl.ds(2 * g + 1, channels, stride=ROWS), :] = turned[1]
        for axis, delta in enumerate((delta_u, delta_v)):
            wave = cos_sin(delta * (0.5 / SUB))
            step = times(wave, wave)
            for j in range(8):
                base_ref[pl.ds(16 * axis + j, channels, stride=BASE), :] = wave[0]
                base_ref[pl.ds(16 * axis + 8 + j, channels, stride=BASE), :] = wave[1]
                if j < 7:
                    wave = times(wave, step)
            for _ in range(3):
                step = times(step, step)
            z_ref[pl.ds(COLUMNS + 2 * axis, channels, stride=ROWS), :] = step[0]
            z_ref[pl.ds(COLUMNS + 2 * axis + 1, channels, stride=ROWS), :] = step[1]
        for c in range(channels):

            def row_of(k):
                return z_ref[ROWS * c + k : ROWS * c + k + 1, :]

            def base_of(k):
                return base_ref[BASE * c + 8 * k : BASE * c + 8 * k + 8, :]

            step = (row_of(COLUMNS), row_of(COLUMNS + 1))
            twice = 2.0 * step[0]
            wave = (base_of(0), base_of(1))
            after = times(wave, step)
            for i in range(COLUMNS):
                for part in range(2):
                    left_ref[c, 128 * part + 16 * i : 128 * part + 16 * i + 16] = jnp.concatenate(
                        [wave[part], after[part]], axis=0
                    ).astype(jnp.bfloat16)
                if i < COLUMNS - 1:
                    wave = tuple(twice * after[part] - wave[part] for part in range(2))
                    after = tuple(twice * wave[part] - after[part] for part in range(2))
            step = (row_of(COLUMNS + 2), row_of(COLUMNS + 3))
            wave = (base_of(2), base_of(3))
            after = times(wave, step)
            both = tuple(jnp.concatenate([wave[part], after[part]], axis=0) for part in range(2))
            for g in range(COLUMNS // 2):
                for part in range(2):
                    turned = row_of(2 * g + part)
                    for kind in range(2):
                        row = 64 * g + 32 * part + 16 * kind
                        right_ref[c, row : row + 16] = (turned * both[kind]).astype(jnp.bfloat16)

    def finish():
        product = None
        for c in range(0, channels, 2):
            right = jnp.concatenate([right_ref[c, 0:256], right_ref[c + 1, 0:256]], axis=1)
            left = jnp.concatenate([left_ref[c, 0:256], left_ref[c + 1, 0:256]], axis=1)
            term = lax.dot_general(right, left, (((1,), (1,)), ((), ())), preferred_element_type=jnp.float32)
            product = term if product is None else product + term
        group = lax.broadcasted_iota(jnp.int32, (HALF, 128), 1) // SUB
        tiles = []
        for sign in (1, -1):
            for g in range(COLUMNS // 2):
                part = [product[64 * g + 16 * k : 64 * g + 16 * k + 16] for k in range(4)]
                (rcc, rcs), (rsc, rss), (icc, ics), (isc, iss) = [(x[:, :128], x[:, 128:]) for x in part]
                kinds = (rcc - sign * ics, -(sign * rss + isc), icc + sign * rcs, rsc - sign * iss)
                tile = None
                for t in range(4):
                    moved = kinds[t] if t == g else pltpu.roll(kinds[t], SUB * ((t - g) % 4), 1)
                    tile = moved if tile is None else jnp.where(group == t, moved, tile)
                facet = facet_row * COLUMNS + (COLUMNS // 2 + g if sign == 1 else COLUMNS // 2 - 1 - g)
                tiles.append((facet ^ me, tile))
        return tiles

    def store(tiles):
        half = block // half_blocks
        row = pl.multiple_of((block - half * half_blocks) * HALF, HALF)

        @pl.when(half == core)
        def _():
            for place, tile in tiles:
                keep_ref[jnp.where(core == 1, swap_low(place), place), pl.ds(row, HALF), :] = tile

        @pl.when(half != core)
        def _():
            for place, tile in tiles:
                send_ref[jnp.where(core == 0, swap_low(place), place), pl.ds(row, HALF), :] = tile

    @pl.when(jnp.logical_or(owners_ref[0] == me, owners_ref[1] == me))
    def _():
        build()
        store(finish())


def grid_blocks(owners, corners, coords, visibilities):
    facet_total = lax.axis_size("facet")
    _, blocks, _, channels, lanes = visibilities.shape
    half_rows = blocks // 2 * HALF
    out = jax.ShapeDtypeStruct((facet_total, half_rows, 128), jnp.float32)
    return pl.pallas_call(
        grid_kernel,
        grid=(facet_total // COLUMNS, blocks),
        in_specs=[pl.BlockSpec(memory_space=pltpu.HBM)] * 4,
        out_specs=[pl.BlockSpec(out.shape, lambda r, b: (0, 0, 0))] * 2,
        scratch_shapes=[
            pltpu.SMEM(owners.shape, jnp.int32),
            pltpu.SMEM(corners.shape, jnp.int32),
            pltpu.VMEM((blocks, 3, 1, lanes), jnp.float32),
            pltpu.VMEM((blocks, 2, channels, lanes), jnp.float32),
            pltpu.SemaphoreType.DMA((3,)),
            pltpu.SemaphoreType.DMA((blocks,)),
            pltpu.VMEM((ROWS * channels, lanes), jnp.float32),
            pltpu.VMEM((BASE * channels, lanes), jnp.float32),
            pltpu.VMEM((channels, 256 + PAD, lanes), jnp.bfloat16),
            pltpu.VMEM((channels, 256 + PAD, lanes), jnp.bfloat16),
        ],
        out_shape=[out, out],
        compiler_params=pltpu.CompilerParams(vmem_limit_bytes=62 * 1024 * 1024),
        name="grid_blocks",
    )(owners, corners, coords.reshape(blocks, 3, 1, lanes), visibilities)


def image_tables(band_total, scale):
    offsets = np.arange(SUB) - HALF
    pixels = np.arange(G) - G // 2
    taper = 1.0 - 0.8 * (offsets / HALF) ** 2
    spread = np.exp(2j * np.pi * np.outer(pixels, offsets) / G)
    table = spread @ np.exp(-2j * np.pi * np.outer(offsets, offsets) / SUB) * taper
    share = G // band_total
    first = np.zeros((2, band_total, 4, SUB, 4, share))
    for sign in range(2):
        for band in range(band_total):
            wave = table[band * share : (band + 1) * share, :: 1 if sign == 0 else -1].T
            for odd in range(2):
                first[sign, band, odd, :, 2 * odd] = wave.real
                first[sign, band, odd, :, 2 * odd + 1] = wave.imag
                first[sign, band, 2 + odd, :, 2 * odd] = -wave.imag
                first[sign, band, 2 + odd, :, 2 * odd + 1] = wave.real
    upper, lower = table.T[HALF:], table.T[HALF - 1 :: -1]
    second = np.stack([(upper + lower).real, (upper + lower).imag, (upper - lower).real, (upper - lower).imag]) * scale
    return first.reshape(2 * band_total, 4 * SUB, 4 * share).astype(np.float32), second.astype(np.float32)


def two_parts(value):
    high = value.astype(jnp.bfloat16)
    return high, (value - high.astype(jnp.float32)).astype(jnp.bfloat16)


def product_of(a, b, dims):
    def dot(x, y):
        return lax.dot_general(x, y, (dims, ((), ())), preferred_element_type=jnp.float32)

    return dot(a[0], b[0]) + (dot(a[0], b[1]) + dot(a[1], b[0]))


def image_kernel(
    table_ref, owners_ref, corners_ref, assign_ref, counts_ref, own_ref, other_ref, first_ref, second_ref, out_ref,
    turn_ref, weight_ref, left_ref, right_ref,
):
    band = lax.axis_index("freq")
    core = band & 1
    blocks = corners_ref.shape[2]
    share, pixels = out_ref.shape[1], out_ref.shape[2]
    half_rows = own_ref.shape[1]
    total = 2 * blocks

    for item in range(total):
        weight_ref[assign_ref[0, item]] = (item < counts_ref[0]).astype(jnp.int32)
    across = lax.broadcasted_iota(jnp.int32, (1, pixels), 1) - pixels // 2
    down = lax.broadcasted_iota(jnp.int32, (1, share), 1) - pixels // 2 + band * share
    for b in range(total):
        owner = owners_ref[b // blocks]
        turn_ref[b : b + 1, 0:pixels] = across * (corners_ref[1, owner, b % blocks] - centre_shift)
        turn_ref[b : b + 1, pixels : pixels + share] = down * (corners_ref[0, owner, b % blocks] - centre_shift)
    turns = (turn_ref[...] & (G - 1)).astype(jnp.float32) * (1.0 / G)
    turn_cos, turn_sin = cos_sin(turns)

    mine = core == 0
    pieces = []
    for s in range(2):
        own, other = own_ref[s], other_ref[s]
        pieces += [jnp.where(mine, own, other), jnp.where(mine, other, own)]
    subs = jnp.concatenate(pieces, axis=0)
    half = product_of(two_parts(subs), two_parts(first_ref[0]), ((1,), (0,)))
    second = [second_ref[k] for k in range(4)]
    for b in range(total):
        weight = weight_ref[b].astype(jnp.float32)
        c, s = turn_cos[b : b + 1, pixels:] * weight, turn_sin[b : b + 1, pixels:] * weight
        rows = half[HALF * b : HALF * b + HALF]
        for odd in range(2):
            real, imag = rows[:, 2 * odd * share : (2 * odd + 1) * share], rows[:, (2 * odd + 1) * share : (2 * odd + 2) * share]
            real, imag = times((real, imag), (c, s))
            for k, value in enumerate((real, imag)):
                at = 4 * HALF * b + (2 * odd + k) * HALF
                high, low = two_parts(value)
                left_ref[0, at : at + HALF] = high
                left_ref[1, at : at + HALF] = low
        c, s = turn_cos[b : b + 1, :pixels], turn_sin[b : b + 1, :pixels]
        for odd in range(2):
            real, imag = times((second[2 * odd], second[2 * odd + 1]), (c, s))
            for k, value in enumerate((real, -imag)):
                at = 4 * HALF * b + (2 * odd + k) * HALF
                high, low = two_parts(value)
                right_ref[0, at : at + HALF] = high
                right_ref[1, at : at + HALF] = low
    out_ref[0] = product_of((left_ref[0], left_ref[1]), (right_ref[0], right_ref[1]), ((0,), (0,)))


def image_blocks(owners, corners, assign, counts, own, other, channel_total, block_rows):
    facet_index, band_index = lax.axis_index("facet"), lax.axis_index("freq")
    band_total = lax.axis_size("freq")
    blocks = corners.shape[2]
    share = G // band_total
    scale = 1.0 / (SUB * SUB * math.sqrt(2 * blocks * block_rows * channel_total))
    first, second = image_tables(band_total, scale)
    left_half = (facet_index % COLUMNS < COLUMNS // 2).astype(jnp.int32)
    table = (left_half * band_total + band_index).reshape(1)
    rows = 2 * blocks * 4 * HALF
    smem = pl.BlockSpec(memory_space=pltpu.SMEM)
    return pl.pallas_call(
        image_kernel,
        grid_spec=pltpu.PrefetchScalarGridSpec(
            num_scalar_prefetch=1,
            grid=(1,),
            in_specs=[
                smem,
                smem,
                smem,
                smem,
                pl.BlockSpec(own.shape, lambda i, t: (0, 0, 0)),
                pl.BlockSpec(own.shape, lambda i, t: (0, 0, 0)),
                pl.BlockSpec((1,) + first.shape[1:], lambda i, t: (t[0], 0, 0)),
                pl.BlockSpec(second.shape, lambda i, t: (0, 0, 0)),
            ],
            out_specs=pl.BlockSpec((1, share, G), lambda i, t: (0, 0, 0)),
            scratch_shapes=[
                pltpu.VMEM((2 * blocks, G + share), jnp.int32),
                pltpu.SMEM((2 * blocks,), jnp.int32),
                pltpu.VMEM((2, rows, share), jnp.bfloat16),
                pltpu.VMEM((2, rows, G), jnp.bfloat16),
            ],
        ),
        out_shape=jax.ShapeDtypeStruct((1, share, G), jnp.float32),
        compiler_params=pltpu.CompilerParams(vmem_limit_bytes=48 * 1024 * 1024),
        name="image_blocks",
    )(table, owners, corners, assign, counts, own, other, jnp.asarray(first), jnp.asarray(second))


def swap(value, partner):
    facet_total, band_total = lax.axis_size("facet"), lax.axis_size("freq")
    pairs = []
    for f in range(facet_total):
        for q in range(band_total):
            to_f, to_q = partner(f, q)
            pairs.append((f * band_total + q, to_f * band_total + to_q))
    return lax.ppermute(value, ("facet", "freq"), pairs)


def on_device(visibilities, coords, corners, owners, assign, counts):
    facet_total, band_total = lax.axis_size("facet"), lax.axis_size("freq")
    facet_index, band_index = lax.axis_index("facet"), lax.axis_index("freq")
    channel_total = visibilities.shape[3] * band_total
    keep, send = grid_blocks(owners, corners, coords, visibilities)
    half_rows = keep.shape[1]
    held = (keep + swap(send, lambda f, q: (f, q ^ 1)))[None]
    for k in range(facet_total.bit_length() - 1):
        even, odd = (k, k ^ 1) if k < 2 else (k, k)
        parts = held.reshape(held.shape[0], -1, 2, half_rows, 128)
        kept, sent = parts[:, :, 0], parts[:, :, 1]
        came = swap(sent, lambda f, q: (f ^ (1 << (odd if q & 1 else even)), q))
        bit = jnp.where(band_index & 1 == 1, odd, even)
        other = ((owners ^ facet_index) >> bit & 1) == 1
        held = jnp.where(other[:, None, None, None], came, kept)
    held = held.reshape(2, half_rows, 128)
    for k in range(1, band_total.bit_length() - 1):
        held = held + swap(held, lambda f, q: (f, q ^ (1 << k)))
    other = swap(held, lambda f, q: (f, q ^ 1))
    return image_blocks(owners, corners, assign, counts, held, other, channel_total, visibilities.shape[4])


def solution(mesh):
    placed = (
        P("facet", None, None, "freq", None),
        P("facet", None, None, None),
        P(),
        P(),
        P("facet", None),
        P("facet"),
    )
    return jax.shard_map(
        on_device, mesh=mesh, in_specs=placed, out_specs=P("facet", "freq", None), check_vma=False
    )
```

```python
import math

import jax
import jax.numpy as jnp
import ml_dtypes
import numpy as np
from jax import lax
from jax.experimental import pallas as pl
from jax.experimental.pallas import tpu as pltpu
from jax.sharding import PartitionSpec as P

SUB = 32
G = 512
HALF = SUB // 2
COLUMNS = 8
ROWS, BASE = 24, 40
PAD = 16

two_pi = 2.0 * math.pi
field_width = 0.02
band_spread = 0.02
centre_shift = G // 2 - SUB // 2

SIN_POLY = (6.2831853, -41.34170041, 81.6051314, -76.70301553, 42.02592778, -14.89984801, 3.23813768)
COS_POLY = (0.99999999, -19.7392045, 64.9391175, -85.45013994, 60.16763282, -25.96760244, 6.52865863)


def poly(square, coefficients):
    total = jnp.full_like(square, coefficients[-1])
    for coefficient in coefficients[-2::-1]:
        total = total * square + coefficient
    return total


def cos_sin(turns):
    rest = turns - jnp.round(turns)
    square = rest * rest
    return poly(square, COS_POLY), rest * poly(square, SIN_POLY)


def times(a, b):
    return a[0] * b[0] - a[1] * b[1], a[0] * b[1] + a[1] * b[0]


def dot(a, b, over):
    return lax.dot_general(a, b, (((1,), (over,)), ((), ())), preferred_element_type=jnp.float32)


def swap_low(value):
    return (value & ~3) | ((value & 1) << 1) | ((value >> 1) & 1)


def grid_kernel(meta_ref, own_ref, other_ref, keep_ref, send_ref, z_ref, base_ref, left_ref, right_ref):
    me = lax.axis_index("facet")
    band = lax.axis_index("freq")
    band_total = lax.axis_size("freq")
    facet_rows = lax.axis_size("facet") // COLUMNS
    core = band & 1
    facet_row = pl.program_id(0)
    step = pl.program_id(1)
    half_blocks = own_ref.shape[0]
    channels, lanes = other_ref.shape[3], other_ref.shape[4]
    block = core * half_blocks + step

    def build(k):
        corner_u = meta_ref[block]
        corner_v = meta_ref[2 * half_blocks + block]
        first_channel = (band ^ k) * channels
        channel = (first_channel + lax.broadcasted_iota(jnp.int32, (channels, lanes), 0)).astype(jnp.float32)
        ratio = 1.0 + band_spread * channel / (channels * band_total)
        u_cells = own_ref[step, 2 * channels : 2 * channels + 1] * ratio
        v_cells = own_ref[step, 2 * channels + 1 : 2 * channels + 2] * ratio
        w_waves = own_ref[step, 2 * channels + 2 : 2 * channels + 3] * ratio
        shift_u = centre_shift - corner_u
        delta_u = u_cells + shift_u.astype(jnp.float32)
        delta_v = v_cells + (centre_shift - corner_v).astype(jnp.float32)
        row_pos = facet_row.astype(jnp.float32) - (facet_rows - 1) / 2.0
        row_vec = jnp.full((8, lanes), row_pos, jnp.float32)
        common = (
            v_cells * row_pos - (delta_u + delta_v) * (0.5 / SUB) + 0.5 * (shift_u & 1).astype(jnp.float32)
        )
        if k == 0:
            vis = (own_ref[step, 0:channels], own_ref[step, channels : 2 * channels])
        else:
            vis = (other_ref[0, block, 0], other_ref[0, block, 1])
        for g in range(COLUMNS // 2):
            radius = field_width * field_width * ((g + 0.5) ** 2 + row_vec * row_vec)
            w_shift = (-radius / (1.0 + jnp.sqrt(1.0 - radius)))[0:1]
            turned = times(vis, cos_sin(common + w_waves * w_shift))
            z_ref[k, pl.ds(2 * g, channels, stride=ROWS), :] = turned[0]
            z_ref[k, pl.ds(2 * g + 1, channels, stride=ROWS), :] = turned[1]
        for axis, delta in enumerate((delta_u, delta_v)):
            wave = cos_sin(delta * (0.5 / SUB))
            turn = times(wave, wave)
            for j in range(8):
                base_ref[k, pl.ds(16 * axis + j, channels, stride=BASE), :] = wave[0]
                base_ref[k, pl.ds(16 * axis + 8 + j, channels, stride=BASE), :] = wave[1]
                if j < 7:
                    wave = times(wave, turn)
            for _ in range(3):
                turn = times(turn, turn)
            z_ref[k, pl.ds(COLUMNS + 2 * axis, channels, stride=ROWS), :] = turn[0]
            z_ref[k, pl.ds(COLUMNS + 2 * axis + 1, channels, stride=ROWS), :] = turn[1]
        for c in range(channels):

            def row_of(i):
                return z_ref[k, ROWS * c + i : ROWS * c + i + 1, :]

            def base_of(i):
                return base_ref[k, BASE * c + 8 * i : BASE * c + 8 * i + 8, :]

            at = k * channels + c
            turn = (row_of(COLUMNS), row_of(COLUMNS + 1))
            twice = 2.0 * turn[0]
            wave = (base_of(0), base_of(1))
            after = times(wave, turn)
            for i in range(COLUMNS):
                for part in range(2):
                    left_ref[at, 128 * part + 16 * i : 128 * part + 16 * i + 16] = jnp.concatenate(
                        [wave[part], after[part]], axis=0
                    ).astype(jnp.bfloat16)
                if i < COLUMNS - 1:
                    wave = tuple(twice * after[part] - wave[part] for part in range(2))
                    after = tuple(twice * wave[part] - after[part] for part in range(2))
            turn = (row_of(COLUMNS + 2), row_of(COLUMNS + 3))
            wave = (base_of(2), base_of(3))
            after = times(wave, turn)
            both = tuple(jnp.concatenate([wave[part], after[part]], axis=0) for part in range(2))
            for g in range(COLUMNS // 2):
                for part in range(2):
                    turned = row_of(2 * g + part)
                    for kind in range(2):
                        row = 64 * g + 32 * part + 16 * kind
                        right_ref[at, row : row + 16] = (turned * both[kind]).astype(jnp.bfloat16)

    def finish():
        product = None
        for c in range(0, 2 * channels, 2):
            right = jnp.concatenate([right_ref[c, 0:256], right_ref[c + 1, 0:256]], axis=1)
            left = jnp.concatenate([left_ref[c, 0:256], left_ref[c + 1, 0:256]], axis=1)
            term = dot(right, left, 1)
            product = term if product is None else product + term
        group = lax.broadcasted_iota(jnp.int32, (HALF, 128), 1) // SUB
        tiles = [None] * COLUMNS
        for sign in (1, -1):
            for g in range(COLUMNS // 2):
                part = [product[64 * g + 16 * k : 64 * g + 16 * k + 16] for k in range(4)]
                (rcc, rcs), (rsc, rss), (icc, ics), (isc, iss) = [(x[:, :128], x[:, 128:]) for x in part]
                kinds = (rcc - sign * ics, -(sign * rss + isc), icc + sign * rcs, rsc - sign * iss)
                tile = None
                for t in range(4):
                    moved = kinds[t] if t == g else pltpu.roll(kinds[t], SUB * ((t - g) % 4), 1)
                    tile = moved if tile is None else jnp.where(group == t, moved, tile)
                tiles[COLUMNS // 2 + g if sign == 1 else COLUMNS // 2 - 1 - g] = tile
        return tiles

    def store(tiles):
        tiles = [jnp.where(core == 1, tiles[swap_low(i)], tiles[i]) if swap_low(i) != i else tiles[i] for i in range(COLUMNS)]
        mine = jnp.where(core == 1, swap_low(me), me)
        row = pl.multiple_of(step * HALF, HALF)
        for i in range(0, COLUMNS, 2):
            place = (facet_row * (COLUMNS // 2) + i // 2) ^ (mine >> 1)
            odd = (mine & 1) == 1
            keep_ref[place, pl.ds(row, HALF), :] = jnp.where(odd, tiles[i + 1], tiles[i])
            send_ref[place, pl.ds(row, HALF), :] = jnp.where(odd, tiles[i], tiles[i + 1])

    owner = 4 * half_blocks

    @pl.when(jnp.logical_or(meta_ref[owner] == me, meta_ref[owner + 1] == me))
    def _():
        build(0)
        build(1)
        store(finish())


def grid_blocks(meta, own, other):
    facet_total = lax.axis_size("facet")
    half_blocks = own.shape[0]
    channels, lanes = other.shape[3:]
    out = jax.ShapeDtypeStruct((facet_total // 2, half_blocks * HALF, 128), jnp.float32)
    vmem = pl.BlockSpec(memory_space=pltpu.VMEM)
    return pl.pallas_call(
        grid_kernel,
        grid=(facet_total // COLUMNS, half_blocks),
        in_specs=[pl.BlockSpec(memory_space=pltpu.SMEM), vmem, vmem],
        out_specs=[vmem, vmem],
        scratch_shapes=[
            pltpu.VMEM((2, ROWS * channels, lanes), jnp.float32),
            pltpu.VMEM((2, BASE * channels, lanes), jnp.float32),
            pltpu.VMEM((2 * channels, 256 + PAD, lanes), jnp.bfloat16),
            pltpu.VMEM((2 * channels, 256 + PAD, lanes), jnp.bfloat16),
        ],
        out_shape=[out, out],
        compiler_params=pltpu.CompilerParams(vmem_limit_bytes=40 * 1024 * 1024),
        name="grid_blocks",
    )(meta, own, other)


def image_tables(band_total, scale):
    offsets = np.arange(SUB) - HALF
    pixels = np.arange(G) - G // 2
    taper = 1.0 - 0.8 * (offsets / HALF) ** 2
    spread = np.exp(2j * np.pi * np.outer(pixels, offsets) / G)
    table = spread @ np.exp(-2j * np.pi * np.outer(offsets, offsets) / SUB) * taper
    share = G // band_total
    first = np.zeros((2, band_total, 4, share, 4, SUB))
    for sign in range(2):
        for band in range(band_total):
            wave = table[band * share : (band + 1) * share, :: 1 if sign == 0 else -1]
            for odd in range(2):
                first[sign, band, 2 * odd, :, odd] = wave.real
                first[sign, band, 2 * odd + 1, :, odd] = wave.imag
                first[sign, band, 2 * odd, :, 2 + odd] = -wave.imag
                first[sign, band, 2 * odd + 1, :, 2 + odd] = wave.real
    first = first.reshape(2 * band_total, 1, 4 * share, 4 * SUB).astype(np.float32)
    high = first.astype(ml_dtypes.bfloat16)
    low = (first - high.astype(np.float32)).astype(ml_dtypes.bfloat16)
    upper, lower = table.T[HALF:], table.T[HALF - 1 :: -1]
    second = np.stack([(upper + lower).real, (upper + lower).imag, (upper - lower).real, (upper - lower).imag]) * scale
    return np.concatenate([high, low], axis=1), second.astype(np.float32)


def two_parts(value):
    high = value.astype(jnp.bfloat16)
    return high, (value - high.astype(jnp.float32)).astype(jnp.bfloat16)


def down_kernel(owners_ref, corners_ref, assign_ref, counts_ref, after_ref, down_ref, weight_ref):
    band = lax.axis_index("freq")
    blocks = corners_ref.shape[2]
    share, rows = down_ref.shape[1:]
    for item in range(2 * blocks):
        weight_ref[assign_ref[0, item]] = (item < counts_ref[0]).astype(jnp.int32)
    group = lax.broadcasted_iota(jnp.int32, (1, rows), 1) // HALF
    corner, weight = jnp.zeros((1, rows), jnp.int32), jnp.zeros((1, rows), jnp.int32)
    for b in range(2 * blocks):
        corner = jnp.where(group == b, corners_ref[0, owners_ref[b // blocks], b % blocks] - centre_shift, corner)
        weight = jnp.where(group == b, weight_ref[b], weight)
    down = lax.broadcasted_iota(jnp.int32, (share, 1), 0) - G // 2 + band * share
    wave = cos_sin(((down * corner) & (G - 1)).astype(jnp.float32) * (1.0 / G))
    for part in range(2):
        down_ref[part] = wave[part] * weight.astype(jnp.float32)


def across_kernel(
    owners_ref, corners_ref, second_ref, tables_ref, after_ref, across_ref, first_ref, turn_ref, first_sem
):
    left_half = (lax.axis_index("facet") % COLUMNS < COLUMNS // 2).astype(jnp.int32)
    index = left_half * lax.axis_size("freq") + lax.axis_index("freq")
    copy = pltpu.make_async_copy(tables_ref.at[index], first_ref, first_sem)
    copy.start()
    blocks = corners_ref.shape[2]
    rows = 2 * blocks * HALF
    pixels = across_ref.shape[2]
    across = lax.broadcasted_iota(jnp.int32, (1, pixels), 1) - pixels // 2
    for b in range(2 * blocks):
        turn_ref[b : b + 1] = across * (corners_ref[1, owners_ref[b // blocks], b % blocks] - centre_shift)
    wave = cos_sin((turn_ref[...] & (G - 1)).astype(jnp.float32) * (1.0 / G))
    full = rows - rows % 128
    for b in range(2 * blocks):
        for odd in range(2):
            real, imag = times((second_ref[2 * odd], second_ref[2 * odd + 1]), (wave[0][b : b + 1], wave[1][b : b + 1]))
            for k, value in enumerate((real, -imag)):
                kind = 2 * odd + k
                at = kind * full + HALF * b if HALF * b < full else 4 * full + kind * (rows - full) + HALF * b - full
                high, low = two_parts(value)
                across_ref[0, at : at + HALF] = high
                across_ref[1, at : at + HALF] = low
    copy.wait()


def image_kernel(own_ref, other_ref, down_ref, across_ref, first_ref, out_ref):
    core = lax.axis_index("freq") & 1
    share = out_ref.shape[1]
    mine = core == 0
    pieces = []
    for s in range(2):
        own, other = own_ref[s], other_ref[s]
        pieces += [jnp.where(mine, own, other), jnp.where(mine, other, own)]
    high, low = two_parts(jnp.concatenate(pieces, axis=0))
    table_high, table_low = first_ref[0], first_ref[1]
    half = dot(table_high, high, 1) + (dot(table_high, low, 1) + dot(table_low, high, 1))
    wave = (down_ref[0], down_ref[1])
    kinds = []
    for odd in range(2):
        at = 2 * odd * share
        kinds += list(times((half[at : at + share], half[at + share : at + 2 * share]), wave))
    rows = half.shape[1]
    full = rows - rows % 128
    pieces = [kind[:, :full] for kind in kinds] + ([kind[:, full:] for kind in kinds] if full < rows else [])
    high, low = two_parts(jnp.concatenate(pieces, axis=1))
    both = dot(jnp.concatenate([high, low], axis=0), across_ref[0], 0)
    out_ref[0] = both[:share] + (both[share:] + dot(high, across_ref[1], 0))


def down_of(owners, corners, assign, counts, after):
    share = G // lax.axis_size("freq")
    total = 2 * corners.shape[2]
    smem = pl.BlockSpec(memory_space=pltpu.SMEM)
    return pl.pallas_call(
        down_kernel,
        in_specs=[smem, smem, smem, smem, pl.BlockSpec(memory_space=pl.ANY)],
        out_specs=pl.BlockSpec(memory_space=pltpu.VMEM),
        out_shape=jax.ShapeDtypeStruct((2, share, total * HALF), jnp.float32),
        scratch_shapes=[pltpu.SMEM((total,), jnp.int32)],
        compiler_params=pltpu.CompilerParams(vmem_limit_bytes=32 * 1024 * 1024),
        cost_estimate=pl.CostEstimate(flops=10**7, bytes_accessed=10**6, transcendentals=0),
        name="image_down",
    )(owners, corners, assign, counts, after)


def across_of(owners, corners, second, first, after):
    total = 2 * corners.shape[2]
    smem, vmem = pl.BlockSpec(memory_space=pltpu.SMEM), pl.BlockSpec(memory_space=pltpu.VMEM)
    return pl.pallas_call(
        across_kernel,
        in_specs=[smem, smem, vmem] + [pl.BlockSpec(memory_space=pl.ANY)] * 2,
        out_specs=[vmem, vmem],
        out_shape=[
            jax.ShapeDtypeStruct((2, 4 * total * HALF, G), jnp.bfloat16),
            jax.ShapeDtypeStruct(first.shape[1:], first.dtype),
        ],
        scratch_shapes=[pltpu.VMEM((total, G), jnp.int32), pltpu.SemaphoreType.DMA(())],
        compiler_params=pltpu.CompilerParams(vmem_limit_bytes=32 * 1024 * 1024),
        cost_estimate=pl.CostEstimate(flops=10**8, bytes_accessed=6 * 10**6, transcendentals=0),
        name="image_across",
    )(owners, corners, second, first, after)


def image_blocks(down, across, first, own, other):
    share, pixels = down.shape[1], across.shape[2]
    return pl.pallas_call(
        image_kernel,
        in_specs=[pl.BlockSpec(memory_space=pltpu.VMEM)] * 5,
        out_specs=pl.BlockSpec(memory_space=pltpu.VMEM),
        out_shape=jax.ShapeDtypeStruct((1, share, pixels), jnp.float32),
        compiler_params=pltpu.CompilerParams(vmem_limit_bytes=40 * 1024 * 1024),
        name="image_blocks",
    )(own, other, down, across, first)


def swap(value, partner):
    facet_total, band_total = lax.axis_size("facet"), lax.axis_size("freq")
    pairs = []
    for f in range(facet_total):
        for q in range(band_total):
            to_f, to_q = partner(f, q)
            pairs.append((f * band_total + q, to_f * band_total + to_q))
    return lax.ppermute(value, ("facet", "freq"), pairs)


def on_device(visibilities, coords, corners, owners, assign, counts):
    facet_total, band_total = lax.axis_size("facet"), lax.axis_size("freq")
    facet_index, band_index = lax.axis_index("facet"), lax.axis_index("freq")
    channel_total = visibilities.shape[3] * band_total
    scale = 1.0 / (SUB * SUB * math.sqrt(2 * corners.shape[2] * visibilities.shape[4] * channel_total))
    first, second = (jnp.asarray(x) for x in image_tables(band_total, scale))
    other = swap(visibilities, lambda f, q: (f, q ^ 1))
    _, blocks, _, channels, lanes = visibilities.shape
    stacked = jnp.concatenate([visibilities[0].reshape(blocks, 2 * channels, lanes), coords[0]], axis=1)
    own = lax.dynamic_slice_in_dim(stacked, (band_index & 1) * (blocks // 2), blocks // 2, 0)
    meta = jnp.concatenate([lax.dynamic_index_in_dim(corners, facet_index, 1, False).reshape(-1), owners])
    meta, own, other = lax.optimization_barrier((meta, own, other))
    kept, sent = grid_blocks(meta, own, other)
    half_rows = kept.shape[1]
    kept, sent = kept[None], sent[None]
    for k in range(facet_total.bit_length() - 1):
        even, odd = (k, k ^ 1) if k < 2 else (k, k)
        if k > 0:
            parts = held.reshape(2, -1, 2, half_rows, 128)
            kept, sent = parts[:, :, 0], parts[:, :, 1]
        tables = ()
        if k == 0:
            tables = down_of(owners, corners, assign, counts, sent)
        if k == 1:
            tables = across_of(owners, corners, second, first, sent)
        came = swap(sent, lambda f, q: (f ^ (1 << (odd if q & 1 else even)), q))
        came, tables = lax.optimization_barrier((came, tables))
        if k == 0:
            down = tables
        if k == 1:
            across, first = tables
        bit = jnp.where(band_index & 1 == 1, odd, even)
        across_bit = ((owners ^ facet_index) >> bit & 1) == 1
        held = jnp.where(across_bit[:, None, None, None], came, kept)
    held = held.reshape(2, half_rows, 128)
    for k in range(1, band_total.bit_length() - 1):
        held = held + swap(held, lambda f, q: (f, q ^ (1 << k)))
    other = swap(held, lambda f, q: (f, q ^ 1))
    return image_blocks(down, across, first, held, other)


def solution(mesh):
    placed = (
        P("facet", None, None, "freq", None),
        P("facet", None, None, None),
        P(),
        P(),
        P("facet", None),
        P("facet"),
    )
    return jax.shard_map(
        on_device, mesh=mesh, in_specs=placed, out_specs=P("facet", "freq", None), check_vma=False
    )
```

```python
import math

import jax
import jax.numpy as jnp
import ml_dtypes
import numpy as np
from jax import lax
from jax.experimental import pallas as pl
from jax.experimental.pallas import tpu as pltpu
from jax.sharding import PartitionSpec as P

SUB = 32
G = 512
HALF = SUB // 2
COLUMNS = 8
BASE = 40
PAD = 16

two_pi = 2.0 * math.pi
field_width = 0.02
band_spread = 0.02
centre_shift = G // 2 - SUB // 2

SIN_POLY = (6.2831853, -41.34170041, 81.6051314, -76.70301553, 42.02592778, -14.89984801, 3.23813768)
COS_POLY = (0.99999999, -19.7392045, 64.9391175, -85.45013994, 60.16763282, -25.96760244, 6.52865863)


def poly(square, coefficients):
    total = jnp.full_like(square, coefficients[-1])
    for coefficient in coefficients[-2::-1]:
        total = total * square + coefficient
    return total


def cos_sin(turns):
    rest = turns - jnp.round(turns)
    square = rest * rest
    return poly(square, COS_POLY), rest * poly(square, SIN_POLY)


def times(a, b):
    return a[0] * b[0] - a[1] * b[1], a[0] * b[1] + a[1] * b[0]


def dot(a, b, over):
    return lax.dot_general(a, b, (((1,), (over,)), ((), ())), preferred_element_type=jnp.float32)


def swap_low(value):
    return (value & ~3) | ((value & 1) << 1) | ((value >> 1) & 1)


def grid_kernel(meta_ref, own_ref, other_ref, keep_ref, send_ref, z_ref, base_ref, left_ref, right_ref):
    me = lax.axis_index("facet")
    band = lax.axis_index("freq")
    band_total = lax.axis_size("freq")
    facet_rows = lax.axis_size("facet") // COLUMNS
    core = band & 1
    facet_row = pl.program_id(0)
    step = pl.program_id(1)
    half_blocks = own_ref.shape[0]
    channels, lanes = other_ref.shape[3], other_ref.shape[4]
    block = core * half_blocks + step

    def build(k):
        corner_u = meta_ref[block]
        corner_v = meta_ref[2 * half_blocks + block]
        first_channel = (band ^ k) * channels
        channel = (first_channel + lax.broadcasted_iota(jnp.int32, (channels, lanes), 0)).astype(jnp.float32)
        ratio = 1.0 + band_spread * channel / (channels * band_total)
        u_cells = own_ref[step, 2 * channels : 2 * channels + 1] * ratio
        v_cells = own_ref[step, 2 * channels + 1 : 2 * channels + 2] * ratio
        w_waves = own_ref[step, 2 * channels + 2 : 2 * channels + 3] * ratio
        shift_u = centre_shift - corner_u
        delta_u = u_cells + shift_u.astype(jnp.float32)
        delta_v = v_cells + (centre_shift - corner_v).astype(jnp.float32)
        row_pos = facet_row.astype(jnp.float32) - (facet_rows - 1) / 2.0
        row_vec = jnp.full((8, lanes), row_pos, jnp.float32)
        common = (
            v_cells * row_pos - (delta_u + delta_v) * (0.5 / SUB) + 0.5 * (shift_u & 1).astype(jnp.float32)
        )
        if k == 0:
            vis = (own_ref[step, 0:channels], own_ref[step, channels : 2 * channels])
        else:
            vis = (other_ref[0, block, 0], other_ref[0, block, 1])
        for g in range(COLUMNS // 2):
            radius = field_width * field_width * ((g + 0.5) ** 2 + row_vec * row_vec)
            w_shift = (-radius / (1.0 + jnp.sqrt(1.0 - radius)))[0:1]
            turned = times(vis, cos_sin(common + w_waves * w_shift))
            z_ref[k, 2 * g, 0:channels] = turned[0]
            z_ref[k, 2 * g + 1, 0:channels] = turned[1]
        for axis, delta in enumerate((delta_u, delta_v)):
            wave = cos_sin(delta * (0.5 / SUB))
            turn = times(wave, wave)
            for j in range(8):
                base_ref[k, pl.ds(16 * axis + j, channels, stride=BASE), :] = wave[0]
                base_ref[k, pl.ds(16 * axis + 8 + j, channels, stride=BASE), :] = wave[1]
                if j == 0:
                    last, wave = wave, times(wave, turn)
                    twice = 2.0 * turn[0]
                elif j < 7:
                    last, wave = wave, tuple(twice * wave[part] - last[part] for part in range(2))
            for _ in range(3):
                turn = times(turn, turn)
            z_ref[k, COLUMNS + 2 * axis, 0:channels] = turn[0]
            z_ref[k, COLUMNS + 2 * axis + 1, 0:channels] = turn[1]
        for c in range(channels):

            def row_of(i):
                return z_ref[k, i, c : c + 1]

            def base_of(i):
                return base_ref[k, BASE * c + 8 * i : BASE * c + 8 * i + 8, :]

            at = k * channels + c
            turn = (row_of(COLUMNS), row_of(COLUMNS + 1))
            twice = 2.0 * turn[0]
            wave = (base_of(0), base_of(1))
            after = times(wave, turn)
            for i in range(COLUMNS):
                for part in range(2):
                    left_ref[at, 128 * part + 16 * i : 128 * part + 16 * i + 16] = jnp.concatenate(
                        [wave[part], after[part]], axis=0
                    ).astype(jnp.bfloat16)
                if i < COLUMNS - 1:
                    wave = tuple(twice * after[part] - wave[part] for part in range(2))
                    after = tuple(twice * wave[part] - after[part] for part in range(2))
            turn = (row_of(COLUMNS + 2), row_of(COLUMNS + 3))
            wave = (base_of(2), base_of(3))
            after = times(wave, turn)
            both = tuple(jnp.concatenate([wave[part], after[part]], axis=0) for part in range(2))
            for g in range(COLUMNS // 2):
                for part in range(2):
                    turned = row_of(2 * g + part)
                    for kind in range(2):
                        row = 64 * g + 32 * part + 16 * kind
                        right_ref[at, row : row + 16] = (turned * both[kind]).astype(jnp.bfloat16)

    def finish():
        product = None
        for c in range(0, 2 * channels, 2):
            right = jnp.concatenate([right_ref[c, 0:256], right_ref[c + 1, 0:256]], axis=1)
            left = jnp.concatenate([left_ref[c, 0:256], left_ref[c + 1, 0:256]], axis=1)
            term = dot(right, left, 1)
            product = term if product is None else product + term
        group = lax.broadcasted_iota(jnp.int32, (HALF, 128), 1) // SUB
        tiles = [None] * COLUMNS
        for sign in (1, -1):
            for g in range(COLUMNS // 2):
                part = [product[64 * g + 16 * k : 64 * g + 16 * k + 16] for k in range(4)]
                (rcc, rcs), (rsc, rss), (icc, ics), (isc, iss) = [(x[:, :128], x[:, 128:]) for x in part]
                kinds = (rcc - sign * ics, -(sign * rss + isc), icc + sign * rcs, rsc - sign * iss)
                tile = None
                for t in range(4):
                    moved = kinds[t] if t == g else pltpu.roll(kinds[t], SUB * ((t - g) % 4), 1)
                    tile = moved if tile is None else jnp.where(group == t, moved, tile)
                tiles[COLUMNS // 2 + g if sign == 1 else COLUMNS // 2 - 1 - g] = tile
        return tiles

    def store(tiles):
        tiles = [jnp.where(core == 1, tiles[swap_low(i)], tiles[i]) if swap_low(i) != i else tiles[i] for i in range(COLUMNS)]
        mine = jnp.where(core == 1, swap_low(me), me)
        row = pl.multiple_of(step * HALF, HALF)
        for i in range(0, COLUMNS, 2):
            place = (facet_row * (COLUMNS // 2) + i // 2) ^ (mine >> 1)
            odd = (mine & 1) == 1
            keep_ref[place, pl.ds(row, HALF), :] = jnp.where(odd, tiles[i + 1], tiles[i])
            send_ref[place, pl.ds(row, HALF), :] = jnp.where(odd, tiles[i], tiles[i + 1])

    owner = 4 * half_blocks

    @pl.when(jnp.logical_or(meta_ref[owner] == me, meta_ref[owner + 1] == me))
    def _():
        build(0)
        build(1)
        store(finish())


def grid_blocks(meta, own, other):
    facet_total = lax.axis_size("facet")
    half_blocks = own.shape[0]
    channels, lanes = other.shape[3:]
    out = jax.ShapeDtypeStruct((facet_total // 2, half_blocks * HALF, 128), jnp.float32)
    vmem = pl.BlockSpec(memory_space=pltpu.VMEM)
    return pl.pallas_call(
        grid_kernel,
        grid=(facet_total // COLUMNS, half_blocks),
        in_specs=[pl.BlockSpec(memory_space=pltpu.SMEM), vmem, vmem],
        out_specs=[vmem, vmem],
        scratch_shapes=[
            pltpu.VMEM((2, COLUMNS + 4, channels + 8, lanes), jnp.float32),
            pltpu.VMEM((2, BASE * channels, lanes), jnp.float32),
            pltpu.VMEM((2 * channels, 256 + PAD, lanes), jnp.bfloat16),
            pltpu.VMEM((2 * channels, 256 + PAD, lanes), jnp.bfloat16),
        ],
        out_shape=[out, out],
        compiler_params=pltpu.CompilerParams(vmem_limit_bytes=40 * 1024 * 1024),
        name="grid_blocks",
    )(meta, own, other)


def image_tables(band_total, scale):
    offsets = np.arange(SUB) - HALF
    pixels = np.arange(G) - G // 2
    taper = 1.0 - 0.8 * (offsets / HALF) ** 2
    spread = np.exp(2j * np.pi * np.outer(pixels, offsets) / G)
    table = spread @ np.exp(-2j * np.pi * np.outer(offsets, offsets) / SUB) * taper
    share = G // band_total
    first = np.zeros((2, band_total, 4, share, 4, SUB))
    for sign in range(2):
        for band in range(band_total):
            wave = table[band * share : (band + 1) * share, :: 1 if sign == 0 else -1]
            for odd in range(2):
                first[sign, band, 2 * odd, :, odd] = wave.real
                first[sign, band, 2 * odd + 1, :, odd] = wave.imag
                first[sign, band, 2 * odd, :, 2 + odd] = -wave.imag
                first[sign, band, 2 * odd + 1, :, 2 + odd] = wave.real
    first = first.reshape(2 * band_total, 1, 4 * share, 4 * SUB).astype(np.float32)
    high = first.astype(ml_dtypes.bfloat16)
    low = (first - high.astype(np.float32)).astype(ml_dtypes.bfloat16)
    upper, lower = table.T[HALF:], table.T[HALF - 1 :: -1]
    second = np.stack([(upper + lower).real, (upper + lower).imag, (upper - lower).real, (upper - lower).imag]) * scale
    return np.concatenate([high, low], axis=1), second.astype(np.float32)


def two_parts(value):
    high = value.astype(jnp.bfloat16)
    return high, (value - high.astype(jnp.float32)).astype(jnp.bfloat16)


def down_kernel(owners_ref, corners_ref, assign_ref, counts_ref, after_ref, down_ref, weight_ref):
    band = lax.axis_index("freq")
    blocks = corners_ref.shape[2]
    share, rows = down_ref.shape[1:]
    for item in range(2 * blocks):
        weight_ref[assign_ref[0, item]] = (item < counts_ref[0]).astype(jnp.int32)
    group = lax.broadcasted_iota(jnp.int32, (1, rows), 1) // HALF
    corner, weight = jnp.zeros((1, rows), jnp.int32), jnp.zeros((1, rows), jnp.int32)
    for b in range(2 * blocks):
        corner = jnp.where(group == b, corners_ref[0, owners_ref[b // blocks], b % blocks] - centre_shift, corner)
        weight = jnp.where(group == b, weight_ref[b], weight)
    down = lax.broadcasted_iota(jnp.int32, (share, 1), 0) - G // 2 + band * share
    wave = cos_sin(((down * corner) & (G - 1)).astype(jnp.float32) * (1.0 / G))
    for part in range(2):
        down_ref[part] = wave[part] * weight.astype(jnp.float32)


def across_kernel(
    owners_ref, corners_ref, second_ref, tables_ref, after_ref, across_ref, first_ref, turn_ref, first_sem
):
    left_half = (lax.axis_index("facet") % COLUMNS < COLUMNS // 2).astype(jnp.int32)
    index = left_half * lax.axis_size("freq") + lax.axis_index("freq")
    copy = pltpu.make_async_copy(tables_ref.at[index], first_ref, first_sem)
    copy.start()
    blocks = corners_ref.shape[2]
    rows = 2 * blocks * HALF
    pixels = across_ref.shape[2]
    across = lax.broadcasted_iota(jnp.int32, (1, pixels), 1) - pixels // 2
    for b in range(2 * blocks):
        turn_ref[b : b + 1] = across * (corners_ref[1, owners_ref[b // blocks], b % blocks] - centre_shift)
    wave = cos_sin((turn_ref[...] & (G - 1)).astype(jnp.float32) * (1.0 / G))
    full = rows - rows % 128
    for b in range(2 * blocks):
        for odd in range(2):
            real, imag = times((second_ref[2 * odd], second_ref[2 * odd + 1]), (wave[0][b : b + 1], wave[1][b : b + 1]))
            for k, value in enumerate((real, -imag)):
                kind = 2 * odd + k
                at = kind * full + HALF * b if HALF * b < full else 4 * full + kind * (rows - full) + HALF * b - full
                high, low = two_parts(value)
                across_ref[0, at : at + HALF] = high
                across_ref[1, at : at + HALF] = low
    copy.wait()


def image_kernel(own_ref, other_ref, down_ref, across_ref, first_ref, out_ref):
    core = lax.axis_index("freq") & 1
    share = out_ref.shape[1]
    mine = core == 0
    pieces = []
    for s in range(2):
        own, other = own_ref[s], other_ref[s]
        pieces += [jnp.where(mine, own, other), jnp.where(mine, other, own)]
    high, low = two_parts(jnp.concatenate(pieces, axis=0))
    table_high, table_low = first_ref[0], first_ref[1]
    half = dot(table_high, high, 1) + (dot(table_high, low, 1) + dot(table_low, high, 1))
    wave = (down_ref[0], down_ref[1])
    kinds = []
    for odd in range(2):
        at = 2 * odd * share
        kinds += list(times((half[at : at + share], half[at + share : at + 2 * share]), wave))
    rows = half.shape[1]
    full = rows - rows % 128
    pieces = [kind[:, :full] for kind in kinds] + ([kind[:, full:] for kind in kinds] if full < rows else [])
    high, low = two_parts(jnp.concatenate(pieces, axis=1))
    both = dot(jnp.concatenate([high, low], axis=0), across_ref[0], 0)
    out_ref[0] = both[:share] + (both[share:] + dot(high, across_ref[1], 0))


def down_of(owners, corners, assign, counts, after):
    share = G // lax.axis_size("freq")
    total = 2 * corners.shape[2]
    smem = pl.BlockSpec(memory_space=pltpu.SMEM)
    return pl.pallas_call(
        down_kernel,
        in_specs=[smem, smem, smem, smem, pl.BlockSpec(memory_space=pl.ANY)],
        out_specs=pl.BlockSpec(memory_space=pltpu.VMEM),
        out_shape=jax.ShapeDtypeStruct((2, share, total * HALF), jnp.float32),
        scratch_shapes=[pltpu.SMEM((total,), jnp.int32)],
        compiler_params=pltpu.CompilerParams(vmem_limit_bytes=32 * 1024 * 1024),
        cost_estimate=pl.CostEstimate(flops=10**7, bytes_accessed=10**6, transcendentals=0),
        name="image_down",
    )(owners, corners, assign, counts, after)


def across_of(owners, corners, second, first, after):
    total = 2 * corners.shape[2]
    smem, vmem = pl.BlockSpec(memory_space=pltpu.SMEM), pl.BlockSpec(memory_space=pltpu.VMEM)
    return pl.pallas_call(
        across_kernel,
        in_specs=[smem, smem, vmem] + [pl.BlockSpec(memory_space=pl.ANY)] * 2,
        out_specs=[vmem, vmem],
        out_shape=[
            jax.ShapeDtypeStruct((2, 4 * total * HALF, G), jnp.bfloat16),
            jax.ShapeDtypeStruct(first.shape[1:], first.dtype),
        ],
        scratch_shapes=[pltpu.VMEM((total, G), jnp.int32), pltpu.SemaphoreType.DMA(())],
        compiler_params=pltpu.CompilerParams(vmem_limit_bytes=32 * 1024 * 1024),
        cost_estimate=pl.CostEstimate(flops=10**8, bytes_accessed=6 * 10**6, transcendentals=0),
        name="image_across",
    )(owners, corners, second, first, after)


def image_blocks(down, across, first, own, other):
    share, pixels = down.shape[1], across.shape[2]
    return pl.pallas_call(
        image_kernel,
        in_specs=[pl.BlockSpec(memory_space=pltpu.VMEM)] * 5,
        out_specs=pl.BlockSpec(memory_space=pltpu.VMEM),
        out_shape=jax.ShapeDtypeStruct((1, share, pixels), jnp.float32),
        compiler_params=pltpu.CompilerParams(vmem_limit_bytes=40 * 1024 * 1024),
        name="image_blocks",
    )(own, other, down, across, first)


def swap(value, partner):
    facet_total, band_total = lax.axis_size("facet"), lax.axis_size("freq")
    pairs = []
    for f in range(facet_total):
        for q in range(band_total):
            to_f, to_q = partner(f, q)
            pairs.append((f * band_total + q, to_f * band_total + to_q))
    return lax.ppermute(value, ("facet", "freq"), pairs)


def on_device(visibilities, coords, corners, owners, assign, counts):
    facet_total, band_total = lax.axis_size("facet"), lax.axis_size("freq")
    facet_index, band_index = lax.axis_index("facet"), lax.axis_index("freq")
    channel_total = visibilities.shape[3] * band_total
    scale = 1.0 / (SUB * SUB * math.sqrt(2 * corners.shape[2] * visibilities.shape[4] * channel_total))
    first, second = (jnp.asarray(x) for x in image_tables(band_total, scale))
    other = swap(visibilities, lambda f, q: (f, q ^ 1))
    _, blocks, _, channels, lanes = visibilities.shape
    stacked = jnp.concatenate([visibilities[0].reshape(blocks, 2 * channels, lanes), coords[0]], axis=1)
    own = lax.dynamic_slice_in_dim(stacked, (band_index & 1) * (blocks // 2), blocks // 2, 0)
    meta = jnp.concatenate([lax.dynamic_index_in_dim(corners, facet_index, 1, False).reshape(-1), owners])
    meta, own, other = lax.optimization_barrier((meta, own, other))
    kept, sent = grid_blocks(meta, own, other)
    half_rows = kept.shape[1]
    kept, sent = kept[None], sent[None]
    for k in range(facet_total.bit_length() - 1):
        even, odd = (k, k ^ 1) if k < 2 else (k, k)
        if k > 0:
            parts = held.reshape(2, -1, 2, half_rows, 128)
            kept, sent = parts[:, :, 0], parts[:, :, 1]
        tables = ()
        if k == 0:
            tables = down_of(owners, corners, assign, counts, sent)
        if k == 1:
            tables = across_of(owners, corners, second, first, sent)
        came = swap(sent, lambda f, q: (f ^ (1 << (odd if q & 1 else even)), q))
        came, tables = lax.optimization_barrier((came, tables))
        if k == 0:
            down = tables
        if k == 1:
            across, first = tables
        bit = jnp.where(band_index & 1 == 1, odd, even)
        across_bit = ((owners ^ facet_index) >> bit & 1) == 1
        held = jnp.where(across_bit[:, None, None, None], came, kept)
    held = held.reshape(2, half_rows, 128)
    for k in range(1, band_total.bit_length() - 1):
        held = held + swap(held, lambda f, q: (f, q ^ (1 << k)))
    other = swap(held, lambda f, q: (f, q ^ 1))
    return image_blocks(down, across, first, held, other)


def solution(mesh):
    placed = (
        P("facet", None, None, "freq", None),
        P("facet", None, None, None),
        P(),
        P(),
        P("facet", None),
        P("facet"),
    )
    return jax.shard_map(
        on_device, mesh=mesh, in_specs=placed, out_specs=P("facet", "freq", None), check_vma=False
    )
```

```python
import math

import jax
import jax.numpy as jnp
import ml_dtypes
import numpy as np
from jax import lax
from jax.experimental import pallas as pl
from jax.experimental.pallas import tpu as pltpu
from jax.sharding import PartitionSpec as P

SUB = 32
G = 512
HALF = SUB // 2
COLUMNS = 8
BASE = 40
PAD = 16

two_pi = 2.0 * math.pi
field_width = 0.02
band_spread = 0.02
centre_shift = G // 2 - SUB // 2

SIN_POLY = (6.2831853, -41.34170041, 81.6051314, -76.70301553, 42.02592778, -14.89984801, 3.23813768)
COS_POLY = (0.99999999, -19.7392045, 64.9391175, -85.45013994, 60.16763282, -25.96760244, 6.52865863)


def poly(square, coefficients):
    total = jnp.full_like(square, coefficients[-1])
    for coefficient in coefficients[-2::-1]:
        total = total * square + coefficient
    return total


def cos_sin(turns):
    rest = turns - jnp.round(turns)
    square = rest * rest
    return poly(square, COS_POLY), rest * poly(square, SIN_POLY)


def times(a, b):
    return a[0] * b[0] - a[1] * b[1], a[0] * b[1] + a[1] * b[0]


def dot(a, b, over):
    return lax.dot_general(a, b, (((1,), (over,)), ((), ())), preferred_element_type=jnp.float32)


def swap_low(value):
    return (value & ~3) | ((value & 1) << 1) | ((value >> 1) & 1)


def gather_kernel(
    owners_hbm, corners_hbm, coords_hbm, vis_hbm, out_ref, owners_ref, corners_ref, coords_ref, sems
):
    me = lax.axis_index("facet")
    half_blocks = out_ref.shape[0]
    first = (lax.axis_index("freq") & 1) * half_blocks
    rows, lanes = vis_hbm.shape[1:]
    ends = (
        (vis_hbm.at[pl.ds(first, half_blocks)], out_ref.at[:, pl.ds(0, rows)]),
        (owners_hbm, owners_ref),
        (corners_hbm, corners_ref),
        (coords_hbm.at[pl.ds(first, half_blocks)], coords_ref),
    )
    copies = [pltpu.make_async_copy(source, target, sems.at[k]) for k, (source, target) in enumerate(ends)]
    for copy in copies:
        copy.start()
    for copy in copies[1:]:
        copy.wait()
    active = jnp.logical_or(owners_ref[0] == me, owners_ref[1] == me).astype(jnp.float32)
    for b in range(half_blocks):
        shifts = [(centre_shift - corners_ref[i, me, first + b]).astype(jnp.float32) for i in range(2)]
        for i, value in enumerate([coords_ref[b, i] for i in range(3)] + shifts + [active]):
            out_ref[b, rows + 8 * i : rows + 8 * i + 8] = jnp.broadcast_to(value, (8, lanes))
    copies[0].wait()


def gather(owners, corners, coords, visibilities):
    _, blocks, _, channels, lanes = visibilities.shape
    rows = 2 * channels
    return pl.pallas_call(
        gather_kernel,
        in_specs=[pl.BlockSpec(memory_space=pltpu.HBM)] * 4,
        out_specs=pl.BlockSpec(memory_space=pltpu.VMEM),
        out_shape=jax.ShapeDtypeStruct((blocks // 2, rows + 48, lanes), jnp.float32),
        scratch_shapes=[
            pltpu.SMEM(owners.shape, jnp.int32),
            pltpu.SMEM(corners.shape, jnp.int32),
            pltpu.VMEM((blocks // 2, 3, 1, lanes), jnp.float32),
            pltpu.SemaphoreType.DMA((4,)),
        ],
        compiler_params=pltpu.CompilerParams(vmem_limit_bytes=60 * 1024 * 1024),
        name="gather_blocks",
    )(owners, corners, coords.reshape(blocks, 3, 1, lanes), visibilities.reshape(blocks, rows, lanes))


def grid_kernel(own_ref, other_ref, keep_ref, send_ref, z_ref, base_ref, left_ref, right_ref):
    me = lax.axis_index("facet")
    band = lax.axis_index("freq")
    band_total = lax.axis_size("freq")
    facet_rows = lax.axis_size("facet") // COLUMNS
    core = band & 1
    facet_row = pl.program_id(0)
    step = pl.program_id(1)
    half_blocks = own_ref.shape[0]
    channels, lanes = other_ref.shape[3], other_ref.shape[4]
    block = core * half_blocks + step

    def build(k):
        first_channel = (band ^ k) * channels
        channel = (first_channel + lax.broadcasted_iota(jnp.int32, (channels, lanes), 0)).astype(jnp.float32)
        ratio = 1.0 + band_spread * channel / (channels * band_total)
        u, v, w, shift_u, shift_v = (own_ref[step, 2 * channels + 8 * i : 2 * channels + 8 * i + 1] for i in range(5))
        u_cells, v_cells, w_waves = u * ratio, v * ratio, w * ratio
        delta_u = u_cells + shift_u
        delta_v = v_cells + shift_v
        half_turn = 0.5 * shift_u - jnp.round(0.5 * shift_u)
        row_pos = facet_row.astype(jnp.float32) - (facet_rows - 1) / 2.0
        row_vec = jnp.full((8, lanes), row_pos, jnp.float32)
        common = v_cells * row_pos - (delta_u + delta_v) * (0.5 / SUB) + half_turn
        if k == 0:
            vis = (own_ref[step, 0:channels], own_ref[step, channels : 2 * channels])
        else:
            vis = (other_ref[0, block, 0], other_ref[0, block, 1])
        for g in range(COLUMNS // 2):
            radius = field_width * field_width * ((g + 0.5) ** 2 + row_vec * row_vec)
            w_shift = (-radius / (1.0 + jnp.sqrt(1.0 - radius)))[0:1]
            turned = times(vis, cos_sin(common + w_waves * w_shift))
            z_ref[k, 2 * g, 0:channels] = turned[0]
            z_ref[k, 2 * g + 1, 0:channels] = turned[1]
        for axis, delta in enumerate((delta_u, delta_v)):
            wave = cos_sin(delta * (0.5 / SUB))
            turn = times(wave, wave)
            for j in range(8):
                base_ref[k, pl.ds(16 * axis + j, channels, stride=BASE), :] = wave[0]
                base_ref[k, pl.ds(16 * axis + 8 + j, channels, stride=BASE), :] = wave[1]
                if j == 0:
                    last, wave = wave, times(wave, turn)
                    twice = 2.0 * turn[0]
                elif j < 7:
                    last, wave = wave, tuple(twice * wave[part] - last[part] for part in range(2))
            for _ in range(3):
                turn = times(turn, turn)
            z_ref[k, COLUMNS + 2 * axis, 0:channels] = turn[0]
            z_ref[k, COLUMNS + 2 * axis + 1, 0:channels] = turn[1]
        for c in range(channels):

            def row_of(i):
                return z_ref[k, i, c : c + 1]

            def base_of(i):
                return base_ref[k, BASE * c + 8 * i : BASE * c + 8 * i + 8, :]

            at = k * channels + c
            turn = (row_of(COLUMNS), row_of(COLUMNS + 1))
            twice = 2.0 * turn[0]
            wave = (base_of(0), base_of(1))
            after = times(wave, turn)
            for i in range(COLUMNS):
                for part in range(2):
                    left_ref[at, 128 * part + 16 * i : 128 * part + 16 * i + 16] = jnp.concatenate(
                        [wave[part], after[part]], axis=0
                    ).astype(jnp.bfloat16)
                if i < COLUMNS - 1:
                    wave = tuple(twice * after[part] - wave[part] for part in range(2))
                    after = tuple(twice * wave[part] - after[part] for part in range(2))
            turn = (row_of(COLUMNS + 2), row_of(COLUMNS + 3))
            wave = (base_of(2), base_of(3))
            after = times(wave, turn)
            both = tuple(jnp.concatenate([wave[part], after[part]], axis=0) for part in range(2))
            for g in range(COLUMNS // 2):
                for part in range(2):
                    turned = row_of(2 * g + part)
                    for kind in range(2):
                        row = 64 * g + 32 * part + 16 * kind
                        right_ref[at, row : row + 16] = (turned * both[kind]).astype(jnp.bfloat16)

    def finish():
        product = None
        for c in range(0, 2 * channels, 2):
            right = jnp.concatenate([right_ref[c, 0:256], right_ref[c + 1, 0:256]], axis=1)
            left = jnp.concatenate([left_ref[c, 0:256], left_ref[c + 1, 0:256]], axis=1)
            term = dot(right, left, 1)
            product = term if product is None else product + term
        group = lax.broadcasted_iota(jnp.int32, (HALF, 128), 1) // SUB
        tiles = [None] * COLUMNS
        for sign in (1, -1):
            for g in range(COLUMNS // 2):
                part = [product[64 * g + 16 * k : 64 * g + 16 * k + 16] for k in range(4)]
                (rcc, rcs), (rsc, rss), (icc, ics), (isc, iss) = [(x[:, :128], x[:, 128:]) for x in part]
                kinds = (rcc - sign * ics, -(sign * rss + isc), icc + sign * rcs, rsc - sign * iss)
                tile = None
                for t in range(4):
                    moved = kinds[t] if t == g else pltpu.roll(kinds[t], SUB * ((t - g) % 4), 1)
                    tile = moved if tile is None else jnp.where(group == t, moved, tile)
                tiles[COLUMNS // 2 + g if sign == 1 else COLUMNS // 2 - 1 - g] = tile
        return tiles

    def store(tiles):
        tiles = [jnp.where(core == 1, tiles[swap_low(i)], tiles[i]) if swap_low(i) != i else tiles[i] for i in range(COLUMNS)]
        mine = jnp.where(core == 1, swap_low(me), me)
        row = pl.multiple_of(step * HALF, HALF)
        for i in range(0, COLUMNS, 2):
            place = (facet_row * (COLUMNS // 2) + i // 2) ^ (mine >> 1)
            odd = (mine & 1) == 1
            keep_ref[place, pl.ds(row, HALF), :] = jnp.where(odd, tiles[i + 1], tiles[i])
            send_ref[place, pl.ds(row, HALF), :] = jnp.where(odd, tiles[i], tiles[i + 1])

    @pl.when(jnp.max(own_ref[step, 2 * channels + 40 : 2 * channels + 48]) > 0.0)
    def _():
        build(0)
        build(1)
        store(finish())


def grid_blocks(own, other):
    facet_total = lax.axis_size("facet")
    half_blocks = own.shape[0]
    channels, lanes = other.shape[3:]
    out = jax.ShapeDtypeStruct((facet_total // 2, half_blocks * HALF, 128), jnp.float32)
    vmem = pl.BlockSpec(memory_space=pltpu.VMEM)
    return pl.pallas_call(
        grid_kernel,
        grid=(facet_total // COLUMNS, half_blocks),
        in_specs=[vmem, vmem],
        out_specs=[vmem, vmem],
        scratch_shapes=[
            pltpu.VMEM((2, COLUMNS + 4, channels + 8, lanes), jnp.float32),
            pltpu.VMEM((2, BASE * channels, lanes), jnp.float32),
            pltpu.VMEM((2 * channels, 256 + PAD, lanes), jnp.bfloat16),
            pltpu.VMEM((2 * channels, 256 + PAD, lanes), jnp.bfloat16),
        ],
        out_shape=[out, out],
        compiler_params=pltpu.CompilerParams(vmem_limit_bytes=40 * 1024 * 1024),
        name="grid_blocks",
    )(own, other)


def image_tables(band_total, scale):
    offsets = np.arange(SUB) - HALF
    pixels = np.arange(G) - G // 2
    taper = 1.0 - 0.8 * (offsets / HALF) ** 2
    spread = np.exp(2j * np.pi * np.outer(pixels, offsets) / G)
    table = spread @ np.exp(-2j * np.pi * np.outer(offsets, offsets) / SUB) * taper
    share = G // band_total
    first = np.zeros((2, band_total, 4, share, 4, SUB))
    for sign in range(2):
        for band in range(band_total):
            wave = table[band * share : (band + 1) * share, :: 1 if sign == 0 else -1]
            for odd in range(2):
                first[sign, band, 2 * odd, :, odd] = wave.real
                first[sign, band, 2 * odd + 1, :, odd] = wave.imag
                first[sign, band, 2 * odd, :, 2 + odd] = -wave.imag
                first[sign, band, 2 * odd + 1, :, 2 + odd] = wave.real
    first = first.reshape(2 * band_total, 1, 4 * share, 4 * SUB).astype(np.float32)
    high = first.astype(ml_dtypes.bfloat16)
    low = (first - high.astype(np.float32)).astype(ml_dtypes.bfloat16)
    upper, lower = table.T[HALF:], table.T[HALF - 1 :: -1]
    second = np.stack([(upper + lower).real, (upper + lower).imag, (upper - lower).real, (upper - lower).imag]) * scale
    return np.concatenate([high, low], axis=1), second.astype(np.float32)


def two_parts(value):
    high = value.astype(jnp.bfloat16)
    return high, (value - high.astype(jnp.float32)).astype(jnp.bfloat16)


def down_kernel(owners_ref, corners_ref, assign_ref, counts_ref, after_ref, down_ref, weight_ref):
    band = lax.axis_index("freq")
    blocks = corners_ref.shape[2]
    share, rows = down_ref.shape[1:]
    for item in range(2 * blocks):
        weight_ref[assign_ref[0, item]] = (item < counts_ref[0]).astype(jnp.int32)
    group = lax.broadcasted_iota(jnp.int32, (1, rows), 1) // HALF
    corner, weight = jnp.zeros((1, rows), jnp.int32), jnp.zeros((1, rows), jnp.int32)
    for b in range(2 * blocks):
        corner = jnp.where(group == b, corners_ref[0, owners_ref[b // blocks], b % blocks] - centre_shift, corner)
        weight = jnp.where(group == b, weight_ref[b], weight)
    down = lax.broadcasted_iota(jnp.int32, (share, 1), 0) - G // 2 + band * share
    wave = cos_sin(((down * corner) & (G - 1)).astype(jnp.float32) * (1.0 / G))
    for part in range(2):
        down_ref[part] = wave[part] * weight.astype(jnp.float32)


def across_kernel(
    owners_ref, corners_ref, second_ref, tables_ref, after_ref, across_ref, first_ref, turn_ref, first_sem
):
    left_half = (lax.axis_index("facet") % COLUMNS < COLUMNS // 2).astype(jnp.int32)
    index = left_half * lax.axis_size("freq") + lax.axis_index("freq")
    copy = pltpu.make_async_copy(tables_ref.at[index], first_ref, first_sem)
    copy.start()
    blocks = corners_ref.shape[2]
    rows = 2 * blocks * HALF
    pixels = across_ref.shape[2]
    across = lax.broadcasted_iota(jnp.int32, (1, pixels), 1) - pixels // 2
    for b in range(2 * blocks):
        turn_ref[b : b + 1] = across * (corners_ref[1, owners_ref[b // blocks], b % blocks] - centre_shift)
    wave = cos_sin((turn_ref[...] & (G - 1)).astype(jnp.float32) * (1.0 / G))
    full = rows - rows % 128
    for b in range(2 * blocks):
        for odd in range(2):
            real, imag = times((second_ref[2 * odd], second_ref[2 * odd + 1]), (wave[0][b : b + 1], wave[1][b : b + 1]))
            for k, value in enumerate((real, -imag)):
                kind = 2 * odd + k
                at = kind * full + HALF * b if HALF * b < full else 4 * full + kind * (rows - full) + HALF * b - full
                high, low = two_parts(value)
                across_ref[0, at : at + HALF] = high
                across_ref[1, at : at + HALF] = low
    copy.wait()


def image_kernel(own_ref, other_ref, down_ref, across_ref, first_ref, out_ref):
    core = lax.axis_index("freq") & 1
    share = out_ref.shape[1]
    mine = core == 0
    pieces = []
    for s in range(2):
        own, other = own_ref[s], other_ref[s]
        pieces += [jnp.where(mine, own, other), jnp.where(mine, other, own)]
    high, low = two_parts(jnp.concatenate(pieces, axis=0))
    table_high, table_low = first_ref[0], first_ref[1]
    half = dot(table_high, high, 1) + (dot(table_high, low, 1) + dot(table_low, high, 1))
    wave = (down_ref[0], down_ref[1])
    kinds = []
    for odd in range(2):
        at = 2 * odd * share
        kinds += list(times((half[at : at + share], half[at + share : at + 2 * share]), wave))
    rows = half.shape[1]
    full = rows - rows % 128
    pieces = [kind[:, :full] for kind in kinds] + ([kind[:, full:] for kind in kinds] if full < rows else [])
    high, low = two_parts(jnp.concatenate(pieces, axis=1))
    both = dot(jnp.concatenate([high, low], axis=0), across_ref[0], 0)
    out_ref[0] = both[:share] + (both[share:] + dot(high, across_ref[1], 0))


def down_of(owners, corners, assign, counts, after):
    share = G // lax.axis_size("freq")
    total = 2 * corners.shape[2]
    smem = pl.BlockSpec(memory_space=pltpu.SMEM)
    return pl.pallas_call(
        down_kernel,
        in_specs=[smem, smem, smem, smem, pl.BlockSpec(memory_space=pl.ANY)],
        out_specs=pl.BlockSpec(memory_space=pltpu.VMEM),
        out_shape=jax.ShapeDtypeStruct((2, share, total * HALF), jnp.float32),
        scratch_shapes=[pltpu.SMEM((total,), jnp.int32)],
        compiler_params=pltpu.CompilerParams(vmem_limit_bytes=32 * 1024 * 1024),
        cost_estimate=pl.CostEstimate(flops=10**7, bytes_accessed=10**6, transcendentals=0),
        name="image_down",
    )(owners, corners, assign, counts, after)


def across_of(owners, corners, second, first, after):
    total = 2 * corners.shape[2]
    smem, vmem = pl.BlockSpec(memory_space=pltpu.SMEM), pl.BlockSpec(memory_space=pltpu.VMEM)
    return pl.pallas_call(
        across_kernel,
        in_specs=[smem, smem, vmem] + [pl.BlockSpec(memory_space=pl.ANY)] * 2,
        out_specs=[vmem, vmem],
        out_shape=[
            jax.ShapeDtypeStruct((2, 4 * total * HALF, G), jnp.bfloat16),
            jax.ShapeDtypeStruct(first.shape[1:], first.dtype),
        ],
        scratch_shapes=[pltpu.VMEM((total, G), jnp.int32), pltpu.SemaphoreType.DMA(())],
        compiler_params=pltpu.CompilerParams(vmem_limit_bytes=32 * 1024 * 1024),
        cost_estimate=pl.CostEstimate(flops=10**8, bytes_accessed=6 * 10**6, transcendentals=0),
        name="image_across",
    )(owners, corners, second, first, after)


def image_blocks(down, across, first, own, other):
    share, pixels = down.shape[1], across.shape[2]
    return pl.pallas_call(
        image_kernel,
        in_specs=[pl.BlockSpec(memory_space=pltpu.VMEM)] * 5,
        out_specs=pl.BlockSpec(memory_space=pltpu.VMEM),
        out_shape=jax.ShapeDtypeStruct((1, share, pixels), jnp.float32),
        compiler_params=pltpu.CompilerParams(vmem_limit_bytes=40 * 1024 * 1024),
        name="image_blocks",
    )(own, other, down, across, first)


def swap(value, partner):
    facet_total, band_total = lax.axis_size("facet"), lax.axis_size("freq")
    pairs = []
    for f in range(facet_total):
        for q in range(band_total):
            to_f, to_q = partner(f, q)
            pairs.append((f * band_total + q, to_f * band_total + to_q))
    return lax.ppermute(value, ("facet", "freq"), pairs)


def on_device(visibilities, coords, corners, owners, assign, counts):
    facet_total, band_total = lax.axis_size("facet"), lax.axis_size("freq")
    facet_index, band_index = lax.axis_index("facet"), lax.axis_index("freq")
    channel_total = visibilities.shape[3] * band_total
    scale = 1.0 / (SUB * SUB * math.sqrt(2 * corners.shape[2] * visibilities.shape[4] * channel_total))
    first, second = (jnp.asarray(x) for x in image_tables(band_total, scale))
    other = swap(visibilities, lambda f, q: (f, q ^ 1))
    own = gather(owners, corners, coords, visibilities)
    kept, sent = grid_blocks(own, other)
    half_rows = kept.shape[1]
    kept, sent = kept[None], sent[None]
    for k in range(facet_total.bit_length() - 1):
        even, odd = (k, k ^ 1) if k < 2 else (k, k)
        if k > 0:
            parts = held.reshape(2, -1, 2, half_rows, 128)
            kept, sent = parts[:, :, 0], parts[:, :, 1]
        tables = ()
        if k == 0:
            tables = down_of(owners, corners, assign, counts, sent)
        if k == 1:
            tables = across_of(owners, corners, second, first, sent)
        came = swap(sent, lambda f, q: (f ^ (1 << (odd if q & 1 else even)), q))
        came, tables = lax.optimization_barrier((came, tables))
        if k == 0:
            down = tables
        if k == 1:
            across, first = tables
        bit = jnp.where(band_index & 1 == 1, odd, even)
        across_bit = ((owners ^ facet_index) >> bit & 1) == 1
        held = jnp.where(across_bit[:, None, None, None], came, kept)
    held = held.reshape(2, half_rows, 128)
    for k in range(1, band_total.bit_length() - 1):
        held = held + swap(held, lambda f, q: (f, q ^ (1 << k)))
    other = swap(held, lambda f, q: (f, q ^ 1))
    return image_blocks(down, across, first, held, other)


def solution(mesh):
    placed = (
        P("facet", None, None, "freq", None),
        P("facet", None, None, None),
        P(),
        P(),
        P("facet", None),
        P("facet"),
    )
    return jax.shard_map(
        on_device, mesh=mesh, in_specs=placed, out_specs=P("facet", "freq", None), check_vma=False
    )
```

```python
import math

import jax
import jax.numpy as jnp
import ml_dtypes
import numpy as np
from jax import lax
from jax.experimental import pallas as pl
from jax.experimental.pallas import tpu as pltpu
from jax.sharding import PartitionSpec as P

SUB = 32
G = 512
HALF = SUB // 2
COLUMNS = 8
BASE = 40
PAD = 16

two_pi = 2.0 * math.pi
field_width = 0.02
band_spread = 0.02
centre_shift = G // 2 - SUB // 2

SIN_POLY = (6.2831853, -41.34170041, 81.6051314, -76.70301553, 42.02592778, -14.89984801, 3.23813768)
COS_POLY = (0.99999999, -19.7392045, 64.9391175, -85.45013994, 60.16763282, -25.96760244, 6.52865863)


def poly(square, coefficients):
    total = jnp.full_like(square, coefficients[-1])
    for coefficient in coefficients[-2::-1]:
        total = total * square + coefficient
    return total


def cos_sin(turns):
    rest = turns - jnp.round(turns)
    square = rest * rest
    return poly(square, COS_POLY), rest * poly(square, SIN_POLY)


def times(a, b):
    return a[0] * b[0] - a[1] * b[1], a[0] * b[1] + a[1] * b[0]


def dot(a, b, over):
    return lax.dot_general(a, b, (((1,), (over,)), ((), ())), preferred_element_type=jnp.float32)


def swap_low(value):
    return (value & ~3) | ((value & 1) << 1) | ((value >> 1) & 1)


def gather_kernel(
    owners_hbm, corners_hbm, coords_hbm, vis_hbm, out_ref, owners_ref, corners_ref, coords_ref, sems
):
    me = lax.axis_index("facet")
    half_blocks = out_ref.shape[0]
    first = (lax.axis_index("freq") & 1) * half_blocks
    rows, lanes = vis_hbm.shape[1:]
    ends = (
        (vis_hbm.at[pl.ds(first, half_blocks)], out_ref.at[:, pl.ds(0, rows)]),
        (owners_hbm, owners_ref),
        (corners_hbm, corners_ref),
        (coords_hbm.at[pl.ds(first, half_blocks)], coords_ref),
    )
    copies = [pltpu.make_async_copy(source, target, sems.at[k]) for k, (source, target) in enumerate(ends)]
    for copy in copies:
        copy.start()
    for copy in copies[1:]:
        copy.wait()
    active = jnp.logical_or(owners_ref[0] == me, owners_ref[1] == me).astype(jnp.float32)
    for b in range(half_blocks):
        shifts = [(centre_shift - corners_ref[i, me, first + b]).astype(jnp.float32) for i in range(2)]
        for i, value in enumerate([coords_ref[b, i] for i in range(3)] + shifts + [active]):
            out_ref[b, rows + 8 * i : rows + 8 * i + 8] = jnp.broadcast_to(value, (8, lanes))
    copies[0].wait()


def gather(owners, corners, coords, visibilities):
    _, blocks, _, channels, lanes = visibilities.shape
    rows = 2 * channels
    return pl.pallas_call(
        gather_kernel,
        in_specs=[pl.BlockSpec(memory_space=pltpu.HBM)] * 4,
        out_specs=pl.BlockSpec(memory_space=pltpu.VMEM),
        out_shape=jax.ShapeDtypeStruct((blocks // 2, rows + 48, lanes), jnp.float32),
        scratch_shapes=[
            pltpu.SMEM(owners.shape, jnp.int32),
            pltpu.SMEM(corners.shape, jnp.int32),
            pltpu.VMEM((blocks // 2, 3, 1, lanes), jnp.float32),
            pltpu.SemaphoreType.DMA((4,)),
        ],
        compiler_params=pltpu.CompilerParams(vmem_limit_bytes=60 * 1024 * 1024),
        name="gather_blocks",
    )(owners, corners, coords.reshape(blocks, 3, 1, lanes), visibilities.reshape(blocks, rows, lanes))


def grid_kernel(own_ref, other_ref, keep_ref, send_ref, z_ref, base_ref, left_ref, right_ref):
    me = lax.axis_index("facet")
    band = lax.axis_index("freq")
    band_total = lax.axis_size("freq")
    facet_rows = lax.axis_size("facet") // COLUMNS
    core = band & 1
    facet_row = pl.program_id(0)
    step = pl.program_id(1)
    half_blocks = own_ref.shape[0]
    channels, lanes = other_ref.shape[3], other_ref.shape[4]
    block = core * half_blocks + step

    def build(k):
        first_channel = (band ^ k) * channels
        channel = (first_channel + lax.broadcasted_iota(jnp.int32, (channels, lanes), 0)).astype(jnp.float32)
        ratio = 1.0 + band_spread * channel / (channels * band_total)
        u, v, w, shift_u, shift_v = (own_ref[step, 2 * channels + 8 * i : 2 * channels + 8 * i + 1] for i in range(5))
        u_cells, v_cells, w_waves = u * ratio, v * ratio, w * ratio
        delta_u = u_cells + shift_u
        delta_v = v_cells + shift_v
        half_turn = 0.5 * shift_u - jnp.round(0.5 * shift_u)
        row_pos = facet_row.astype(jnp.float32) - (facet_rows - 1) / 2.0
        row_vec = jnp.full((8, lanes), row_pos, jnp.float32)
        common = v_cells * row_pos - (delta_u + delta_v) * (0.5 / SUB) + half_turn
        if k == 0:
            vis = (own_ref[step, 0:channels], own_ref[step, channels : 2 * channels])
        else:
            vis = (other_ref[0, block, 0], other_ref[0, block, 1])
        for g in range(COLUMNS // 2):
            radius = field_width * field_width * ((g + 0.5) ** 2 + row_vec * row_vec)
            w_shift = (-radius / (1.0 + jnp.sqrt(1.0 - radius)))[0:1]
            turned = times(vis, cos_sin(common + w_waves * w_shift))
            z_ref[k, 2 * g, 0:channels] = turned[0]
            z_ref[k, 2 * g + 1, 0:channels] = turned[1]
        for axis, delta in enumerate((delta_u, delta_v)):
            wave = cos_sin(delta * (0.5 / SUB))
            turn = times(wave, wave)
            for j in range(8):
                base_ref[k, pl.ds(16 * axis + j, channels, stride=BASE), :] = wave[0]
                base_ref[k, pl.ds(16 * axis + 8 + j, channels, stride=BASE), :] = wave[1]
                if j == 0:
                    last, wave = wave, times(wave, turn)
                    twice = 2.0 * turn[0]
                elif j < 7:
                    last, wave = wave, tuple(twice * wave[part] - last[part] for part in range(2))
            for _ in range(3):
                turn = times(turn, turn)
            z_ref[k, COLUMNS + 2 * axis, 0:channels] = turn[0]
            z_ref[k, COLUMNS + 2 * axis + 1, 0:channels] = turn[1]

    def add_rows(k, c):
        def row_of(i):
            return z_ref[k, i, c : c + 1]

        def base_of(i):
            return base_ref[k, BASE * c + 8 * i : BASE * c + 8 * i + 8, :]

        at = k * channels + c
        turn = (row_of(COLUMNS), row_of(COLUMNS + 1))
        twice = 2.0 * turn[0]
        wave = (base_of(0), base_of(1))
        after = times(wave, turn)
        for i in range(COLUMNS):
            for part in range(2):
                left_ref[at, 128 * part + 16 * i : 128 * part + 16 * i + 16] = jnp.concatenate(
                    [wave[part], after[part]], axis=0
                ).astype(jnp.bfloat16)
            if i < COLUMNS - 1:
                wave = tuple(twice * after[part] - wave[part] for part in range(2))
                after = tuple(twice * wave[part] - after[part] for part in range(2))
        turn = (row_of(COLUMNS + 2), row_of(COLUMNS + 3))
        wave = (base_of(2), base_of(3))
        after = times(wave, turn)
        both = tuple(jnp.concatenate([wave[part], after[part]], axis=0) for part in range(2))
        for g in range(COLUMNS // 2):
            for part in range(2):
                turned = row_of(2 * g + part)
                for kind in range(2):
                    row = 64 * g + 32 * part + 16 * kind
                    right_ref[at, row : row + 16] = (turned * both[kind]).astype(jnp.bfloat16)

    def finish(product):
        group = lax.broadcasted_iota(jnp.int32, (HALF, 128), 1) // SUB
        tiles = [None] * COLUMNS
        for sign in (1, -1):
            for g in range(COLUMNS // 2):
                part = [product[64 * g + 16 * k : 64 * g + 16 * k + 16] for k in range(4)]
                (rcc, rcs), (rsc, rss), (icc, ics), (isc, iss) = [(x[:, :128], x[:, 128:]) for x in part]
                kinds = (rcc - sign * ics, -(sign * rss + isc), icc + sign * rcs, rsc - sign * iss)
                tile = None
                for t in range(4):
                    moved = kinds[t] if t == g else pltpu.roll(kinds[t], SUB * ((t - g) % 4), 1)
                    tile = moved if tile is None else jnp.where(group == t, moved, tile)
                tiles[COLUMNS // 2 + g if sign == 1 else COLUMNS // 2 - 1 - g] = tile
        return tiles

    def store(tiles):
        tiles = [jnp.where(core == 1, tiles[swap_low(i)], tiles[i]) if swap_low(i) != i else tiles[i] for i in range(COLUMNS)]
        mine = jnp.where(core == 1, swap_low(me), me)
        row = pl.multiple_of(step * HALF, HALF)
        for i in range(0, COLUMNS, 2):
            place = (facet_row * (COLUMNS // 2) + i // 2) ^ (mine >> 1)
            odd = (mine & 1) == 1
            keep_ref[place, pl.ds(row, HALF), :] = jnp.where(odd, tiles[i + 1], tiles[i])
            send_ref[place, pl.ds(row, HALF), :] = jnp.where(odd, tiles[i], tiles[i + 1])

    @pl.when(jnp.max(own_ref[step, 2 * channels + 40 : 2 * channels + 48]) > 0.0)
    def _():
        build(0)
        product = None
        for c in range(0, 2 * channels, 2):
            if c == channels // 2:
                build(1)
            for i in range(2):
                add_rows(c // channels, c % channels + i)
            right = jnp.concatenate([right_ref[c, 0:256], right_ref[c + 1, 0:256]], axis=1)
            left = jnp.concatenate([left_ref[c, 0:256], left_ref[c + 1, 0:256]], axis=1)
            term = dot(right, left, 1)
            product = term if product is None else product + term
        store(finish(product))


def grid_blocks(own, other):
    facet_total = lax.axis_size("facet")
    half_blocks = own.shape[0]
    channels, lanes = other.shape[3:]
    out = jax.ShapeDtypeStruct((facet_total // 2, half_blocks * HALF, 128), jnp.float32)
    vmem = pl.BlockSpec(memory_space=pltpu.VMEM)
    return pl.pallas_call(
        grid_kernel,
        grid=(facet_total // COLUMNS, half_blocks),
        in_specs=[vmem, vmem],
        out_specs=[vmem, vmem],
        scratch_shapes=[
            pltpu.VMEM((2, COLUMNS + 4, channels + 8, lanes), jnp.float32),
            pltpu.VMEM((2, BASE * channels, lanes), jnp.float32),
            pltpu.VMEM((2 * channels, 256 + PAD, lanes), jnp.bfloat16),
            pltpu.VMEM((2 * channels, 256 + PAD, lanes), jnp.bfloat16),
        ],
        out_shape=[out, out],
        compiler_params=pltpu.CompilerParams(vmem_limit_bytes=40 * 1024 * 1024),
        name="grid_blocks",
    )(own, other)


def image_tables(band_total, scale):
    offsets = np.arange(SUB) - HALF
    pixels = np.arange(G) - G // 2
    taper = 1.0 - 0.8 * (offsets / HALF) ** 2
    spread = np.exp(2j * np.pi * np.outer(pixels, offsets) / G)
    table = spread @ np.exp(-2j * np.pi * np.outer(offsets, offsets) / SUB) * taper
    share = G // band_total
    first = np.zeros((2, band_total, 4, share, 4, SUB))
    for sign in range(2):
        for band in range(band_total):
            wave = table[band * share : (band + 1) * share, :: 1 if sign == 0 else -1]
            for odd in range(2):
                first[sign, band, 2 * odd, :, odd] = wave.real
                first[sign, band, 2 * odd + 1, :, odd] = wave.imag
                first[sign, band, 2 * odd, :, 2 + odd] = -wave.imag
                first[sign, band, 2 * odd + 1, :, 2 + odd] = wave.real
    first = first.reshape(2 * band_total, 1, 4 * share, 4 * SUB).astype(np.float32)
    high = first.astype(ml_dtypes.bfloat16)
    low = (first - high.astype(np.float32)).astype(ml_dtypes.bfloat16)
    upper, lower = table.T[HALF:], table.T[HALF - 1 :: -1]
    second = np.stack([(upper + lower).real, (upper + lower).imag, (upper - lower).real, (upper - lower).imag]) * scale
    return np.concatenate([high, low], axis=1), second.astype(np.float32)


def two_parts(value):
    high = value.astype(jnp.bfloat16)
    return high, (value - high.astype(jnp.float32)).astype(jnp.bfloat16)


def down_kernel(owners_ref, corners_ref, assign_ref, counts_ref, after_ref, down_ref, weight_ref):
    band = lax.axis_index("freq")
    blocks = corners_ref.shape[2]
    share, rows = down_ref.shape[1:]
    for item in range(2 * blocks):
        weight_ref[assign_ref[0, item]] = (item < counts_ref[0]).astype(jnp.int32)
    group = lax.broadcasted_iota(jnp.int32, (1, rows), 1) // HALF
    corner, weight = jnp.zeros((1, rows), jnp.int32), jnp.zeros((1, rows), jnp.int32)
    for b in range(2 * blocks):
        corner = jnp.where(group == b, corners_ref[0, owners_ref[b // blocks], b % blocks] - centre_shift, corner)
        weight = jnp.where(group == b, weight_ref[b], weight)
    down = lax.broadcasted_iota(jnp.int32, (share, 1), 0) - G // 2 + band * share
    wave = cos_sin(((down * corner) & (G - 1)).astype(jnp.float32) * (1.0 / G))
    for part in range(2):
        down_ref[part] = wave[part] * weight.astype(jnp.float32)


def across_kernel(
    owners_ref, corners_ref, second_ref, tables_ref, after_ref, across_ref, first_ref, turn_ref, first_sem
):
    left_half = (lax.axis_index("facet") % COLUMNS < COLUMNS // 2).astype(jnp.int32)
    index = left_half * lax.axis_size("freq") + lax.axis_index("freq")
    copy = pltpu.make_async_copy(tables_ref.at[index], first_ref, first_sem)
    copy.start()
    blocks = corners_ref.shape[2]
    rows = 2 * blocks * HALF
    pixels = across_ref.shape[2]
    across = lax.broadcasted_iota(jnp.int32, (1, pixels), 1) - pixels // 2
    for b in range(2 * blocks):
        turn_ref[b : b + 1] = across * (corners_ref[1, owners_ref[b // blocks], b % blocks] - centre_shift)
    wave = cos_sin((turn_ref[...] & (G - 1)).astype(jnp.float32) * (1.0 / G))
    full = rows - rows % 128
    for b in range(2 * blocks):
        for odd in range(2):
            real, imag = times((second_ref[2 * odd], second_ref[2 * odd + 1]), (wave[0][b : b + 1], wave[1][b : b + 1]))
            for k, value in enumerate((real, -imag)):
                kind = 2 * odd + k
                at = kind * full + HALF * b if HALF * b < full else 4 * full + kind * (rows - full) + HALF * b - full
                high, low = two_parts(value)
                across_ref[0, at : at + HALF] = high
                across_ref[1, at : at + HALF] = low
    copy.wait()


def image_kernel(own_ref, other_ref, down_ref, across_ref, first_ref, out_ref):
    core = lax.axis_index("freq") & 1
    share = out_ref.shape[1]
    mine = core == 0
    pieces = []
    for s in range(2):
        own, other = own_ref[s], other_ref[s]
        pieces += [jnp.where(mine, own, other), jnp.where(mine, other, own)]
    high, low = two_parts(jnp.concatenate(pieces, axis=0))
    table_high, table_low = first_ref[0], first_ref[1]
    half = dot(table_high, high, 1) + (dot(table_high, low, 1) + dot(table_low, high, 1))
    wave = (down_ref[0], down_ref[1])
    kinds = []
    for odd in range(2):
        at = 2 * odd * share
        kinds += list(times((half[at : at + share], half[at + share : at + 2 * share]), wave))
    rows = half.shape[1]
    full = rows - rows % 128
    pieces = [kind[:, :full] for kind in kinds] + ([kind[:, full:] for kind in kinds] if full < rows else [])
    high, low = two_parts(jnp.concatenate(pieces, axis=1))
    both = dot(jnp.concatenate([high, low], axis=0), across_ref[0], 0)
    out_ref[0] = both[:share] + (both[share:] + dot(high, across_ref[1], 0))


def down_of(owners, corners, assign, counts, after):
    share = G // lax.axis_size("freq")
    total = 2 * corners.shape[2]
    smem = pl.BlockSpec(memory_space=pltpu.SMEM)
    return pl.pallas_call(
        down_kernel,
        in_specs=[smem, smem, smem, smem, pl.BlockSpec(memory_space=pl.ANY)],
        out_specs=pl.BlockSpec(memory_space=pltpu.VMEM),
        out_shape=jax.ShapeDtypeStruct((2, share, total * HALF), jnp.float32),
        scratch_shapes=[pltpu.SMEM((total,), jnp.int32)],
        compiler_params=pltpu.CompilerParams(vmem_limit_bytes=32 * 1024 * 1024),
        cost_estimate=pl.CostEstimate(flops=10**7, bytes_accessed=10**6, transcendentals=0),
        name="image_down",
    )(owners, corners, assign, counts, after)


def across_of(owners, corners, second, first, after):
    total = 2 * corners.shape[2]
    smem, vmem = pl.BlockSpec(memory_space=pltpu.SMEM), pl.BlockSpec(memory_space=pltpu.VMEM)
    return pl.pallas_call(
        across_kernel,
        in_specs=[smem, smem, vmem] + [pl.BlockSpec(memory_space=pl.ANY)] * 2,
        out_specs=[vmem, vmem],
        out_shape=[
            jax.ShapeDtypeStruct((2, 4 * total * HALF, G), jnp.bfloat16),
            jax.ShapeDtypeStruct(first.shape[1:], first.dtype),
        ],
        scratch_shapes=[pltpu.VMEM((total, G), jnp.int32), pltpu.SemaphoreType.DMA(())],
        compiler_params=pltpu.CompilerParams(vmem_limit_bytes=32 * 1024 * 1024),
        cost_estimate=pl.CostEstimate(flops=10**8, bytes_accessed=6 * 10**6, transcendentals=0),
        name="image_across",
    )(owners, corners, second, first, after)


def image_blocks(down, across, first, own, other):
    share, pixels = down.shape[1], across.shape[2]
    return pl.pallas_call(
        image_kernel,
        in_specs=[pl.BlockSpec(memory_space=pltpu.VMEM)] * 5,
        out_specs=pl.BlockSpec(memory_space=pltpu.VMEM),
        out_shape=jax.ShapeDtypeStruct((1, share, pixels), jnp.float32),
        compiler_params=pltpu.CompilerParams(vmem_limit_bytes=40 * 1024 * 1024),
        name="image_blocks",
    )(own, other, down, across, first)


def swap(value, partner):
    facet_total, band_total = lax.axis_size("facet"), lax.axis_size("freq")
    pairs = []
    for f in range(facet_total):
        for q in range(band_total):
            to_f, to_q = partner(f, q)
            pairs.append((f * band_total + q, to_f * band_total + to_q))
    return lax.ppermute(value, ("facet", "freq"), pairs)


def on_device(visibilities, coords, corners, owners, assign, counts):
    facet_total, band_total = lax.axis_size("facet"), lax.axis_size("freq")
    facet_index, band_index = lax.axis_index("facet"), lax.axis_index("freq")
    channel_total = visibilities.shape[3] * band_total
    scale = 1.0 / (SUB * SUB * math.sqrt(2 * corners.shape[2] * visibilities.shape[4] * channel_total))
    first, second = (jnp.asarray(x) for x in image_tables(band_total, scale))
    other = swap(visibilities, lambda f, q: (f, q ^ 1))
    own = gather(owners, corners, coords, visibilities)
    kept, sent = grid_blocks(own, other)
    half_rows = kept.shape[1]
    kept, sent = kept[None], sent[None]
    for k in range(facet_total.bit_length() - 1):
        even, odd = (k, k ^ 1) if k < 2 else (k, k)
        if k > 0:
            parts = held.reshape(2, -1, 2, half_rows, 128)
            kept, sent = parts[:, :, 0], parts[:, :, 1]
        tables = ()
        if k == 0:
            tables = down_of(owners, corners, assign, counts, sent)
        if k == 1:
            tables = across_of(owners, corners, second, first, sent)
        came = swap(sent, lambda f, q: (f ^ (1 << (odd if q & 1 else even)), q))
        came, tables = lax.optimization_barrier((came, tables))
        if k == 0:
            down = tables
        if k == 1:
            across, first = tables
        bit = jnp.where(band_index & 1 == 1, odd, even)
        across_bit = ((owners ^ facet_index) >> bit & 1) == 1
        held = jnp.where(across_bit[:, None, None, None], came, kept)
    held = held.reshape(2, half_rows, 128)
    for k in range(1, band_total.bit_length() - 1):
        held = held + swap(held, lambda f, q: (f, q ^ (1 << k)))
    other = swap(held, lambda f, q: (f, q ^ 1))
    return image_blocks(down, across, first, held, other)


def solution(mesh):
    placed = (
        P("facet", None, None, "freq", None),
        P("facet", None, None, None),
        P(),
        P(),
        P("facet", None),
        P("facet"),
    )
    return jax.shard_map(
        on_device, mesh=mesh, in_specs=placed, out_specs=P("facet", "freq", None), check_vma=False
    )
```

```python
import math

import jax
import jax.numpy as jnp
import ml_dtypes
import numpy as np
from jax import lax
from jax.experimental import pallas as pl
from jax.experimental.pallas import tpu as pltpu
from jax.sharding import PartitionSpec as P

SUB = 32
G = 512
HALF = SUB // 2
COLUMNS = 8
BASE = 56
PAD = 16

two_pi = 2.0 * math.pi
field_width = 0.02
band_spread = 0.02
centre_shift = G // 2 - SUB // 2

SIN_POLY = (6.2831853, -41.34170041, 81.6051314, -76.70301553, 42.02592778, -14.89984801, 3.23813768)
COS_POLY = (0.99999999, -19.7392045, 64.9391175, -85.45013994, 60.16763282, -25.96760244, 6.52865863)


def poly(square, coefficients):
    total = jnp.full_like(square, coefficients[-1])
    for coefficient in coefficients[-2::-1]:
        total = total * square + coefficient
    return total


def cos_sin(turns):
    rest = turns - jnp.round(turns)
    square = rest * rest
    return poly(square, COS_POLY), rest * poly(square, SIN_POLY)


def times(a, b):
    return a[0] * b[0] - a[1] * b[1], a[0] * b[1] + a[1] * b[0]


def dot(a, b, over):
    return lax.dot_general(a, b, (((1,), (over,)), ((), ())), preferred_element_type=jnp.float32)


def swap_low(value):
    return (value & ~3) | ((value & 1) << 1) | ((value >> 1) & 1)


def gather_kernel(
    owners_hbm, corners_hbm, coords_hbm, vis_hbm, out_ref, owners_ref, corners_ref, coords_ref, sems
):
    me = lax.axis_index("facet")
    half_blocks = out_ref.shape[0]
    first = (lax.axis_index("freq") & 1) * half_blocks
    rows, lanes = vis_hbm.shape[1:]
    ends = (
        (vis_hbm.at[pl.ds(first, half_blocks)], out_ref.at[:, pl.ds(0, rows)]),
        (owners_hbm, owners_ref),
        (corners_hbm, corners_ref),
        (coords_hbm.at[pl.ds(first, half_blocks)], coords_ref),
    )
    copies = [pltpu.make_async_copy(source, target, sems.at[k]) for k, (source, target) in enumerate(ends)]
    for copy in copies:
        copy.start()
    for copy in copies[1:]:
        copy.wait()
    active = jnp.logical_or(owners_ref[0] == me, owners_ref[1] == me).astype(jnp.float32)
    for b in range(half_blocks):
        shifts = [(centre_shift - corners_ref[i, me, first + b]).astype(jnp.float32) for i in range(2)]
        for i, value in enumerate([coords_ref[b, i] for i in range(3)] + shifts + [active]):
            out_ref[b, rows + 8 * i : rows + 8 * i + 8] = jnp.broadcast_to(value, (8, lanes))
    copies[0].wait()


def gather(owners, corners, coords, visibilities):
    _, blocks, _, channels, lanes = visibilities.shape
    rows = 2 * channels
    return pl.pallas_call(
        gather_kernel,
        in_specs=[pl.BlockSpec(memory_space=pltpu.HBM)] * 4,
        out_specs=pl.BlockSpec(memory_space=pltpu.VMEM),
        out_shape=jax.ShapeDtypeStruct((blocks // 2, rows + 48, lanes), jnp.float32),
        scratch_shapes=[
            pltpu.SMEM(owners.shape, jnp.int32),
            pltpu.SMEM(corners.shape, jnp.int32),
            pltpu.VMEM((blocks // 2, 3, 1, lanes), jnp.float32),
            pltpu.SemaphoreType.DMA((4,)),
        ],
        compiler_params=pltpu.CompilerParams(vmem_limit_bytes=60 * 1024 * 1024),
        name="gather_blocks",
    )(owners, corners, coords.reshape(blocks, 3, 1, lanes), visibilities.reshape(blocks, rows, lanes))


def grid_kernel(own_ref, other_ref, keep_ref, send_ref, z_ref, base_ref, left_ref, right_ref):
    me = lax.axis_index("facet")
    band = lax.axis_index("freq")
    band_total = lax.axis_size("freq")
    facet_rows = lax.axis_size("facet") // COLUMNS
    core = band & 1
    facet_row = pl.program_id(0)
    step = pl.program_id(1)
    half_blocks = own_ref.shape[0]
    channels, lanes = other_ref.shape[3], other_ref.shape[4]
    block = core * half_blocks + step

    def build(k):
        first_channel = (band ^ k) * channels
        channel = (first_channel + lax.broadcasted_iota(jnp.int32, (channels, lanes), 0)).astype(jnp.float32)
        ratio = 1.0 + band_spread * channel / (channels * band_total)
        u, v, w, shift_u, shift_v = (own_ref[step, 2 * channels + 8 * i : 2 * channels + 8 * i + 1] for i in range(5))
        u_cells, v_cells, w_waves = u * ratio, v * ratio, w * ratio
        delta_u = u_cells + shift_u
        delta_v = v_cells + shift_v
        half_turn = 0.5 * shift_u - jnp.round(0.5 * shift_u)
        row_pos = facet_row.astype(jnp.float32) - (facet_rows - 1) / 2.0
        row_vec = jnp.full((8, lanes), row_pos, jnp.float32)
        common = v_cells * row_pos - (delta_u + delta_v) * (0.5 / SUB) + half_turn
        if k == 0:
            vis = (own_ref[step, 0:channels], own_ref[step, channels : 2 * channels])
        else:
            vis = (other_ref[0, block, 0], other_ref[0, block, 1])
        for g in range(COLUMNS // 2):
            radius = field_width * field_width * ((g + 0.5) ** 2 + row_vec * row_vec)
            w_shift = (-radius / (1.0 + jnp.sqrt(1.0 - radius)))[0:1]
            turned = times(vis, cos_sin(common + w_waves * w_shift))
            z_ref[k, 2 * g, 0:channels] = turned[0]
            z_ref[k, 2 * g + 1, 0:channels] = turned[1]
        for axis, delta in enumerate((delta_u, delta_v)):
            wave = cos_sin(delta * (0.5 / SUB))
            turn = times(wave, wave)
            count = 8 + 8 * axis
            for j in range(count):
                base_ref[k, pl.ds(16 * axis + j, channels, stride=BASE), :] = wave[0]
                base_ref[k, pl.ds(16 * axis + count + j, channels, stride=BASE), :] = wave[1]
                if j == 0:
                    last, wave = wave, times(wave, turn)
                    twice = 2.0 * turn[0]
                elif j < count - 1:
                    last, wave = wave, tuple(twice * wave[part] - last[part] for part in range(2))
            if axis == 1:
                break
            for _ in range(3):
                turn = times(turn, turn)
            z_ref[k, COLUMNS + 2 * axis, 0:channels] = turn[0]
            z_ref[k, COLUMNS + 2 * axis + 1, 0:channels] = turn[1]

    def add_rows(k, c):
        def row_of(i):
            return z_ref[k, i, c : c + 1]

        def base_of(i):
            return base_ref[k, BASE * c + 8 * i : BASE * c + 8 * i + 8, :]

        at = k * channels + c
        turn = (row_of(COLUMNS), row_of(COLUMNS + 1))
        twice = 2.0 * turn[0]
        wave = (base_of(0), base_of(1))
        after = times(wave, turn)
        for i in range(COLUMNS):
            for part in range(2):
                left_ref[at, 128 * part + 16 * i : 128 * part + 16 * i + 16] = jnp.concatenate(
                    [wave[part], after[part]], axis=0
                ).astype(jnp.bfloat16)
            if i < COLUMNS - 1:
                wave = tuple(twice * after[part] - wave[part] for part in range(2))
                after = tuple(twice * wave[part] - after[part] for part in range(2))
        both = tuple(base_ref[k, BASE * c + 16 + 16 * i : BASE * c + 32 + 16 * i, :] for i in range(2))
        for g in range(COLUMNS // 2):
            for part in range(2):
                turned = row_of(2 * g + part)
                for kind in range(2):
                    row = 64 * g + 32 * part + 16 * kind
                    right_ref[at, row : row + 16] = (turned * both[kind]).astype(jnp.bfloat16)

    def finish(product):
        group = lax.broadcasted_iota(jnp.int32, (HALF, 128), 1) // SUB
        tiles = [None] * COLUMNS
        for sign in (1, -1):
            for g in range(COLUMNS // 2):
                part = [product[64 * g + 16 * k : 64 * g + 16 * k + 16] for k in range(4)]
                (rcc, rcs), (rsc, rss), (icc, ics), (isc, iss) = [(x[:, :128], x[:, 128:]) for x in part]
                kinds = (rcc - sign * ics, -(sign * rss + isc), icc + sign * rcs, rsc - sign * iss)
                tile = None
                for t in range(4):
                    moved = kinds[t] if t == g else pltpu.roll(kinds[t], SUB * ((t - g) % 4), 1)
                    tile = moved if tile is None else jnp.where(group == t, moved, tile)
                tiles[COLUMNS // 2 + g if sign == 1 else COLUMNS // 2 - 1 - g] = tile
        return tiles

    def store(tiles):
        tiles = [jnp.where(core == 1, tiles[swap_low(i)], tiles[i]) if swap_low(i) != i else tiles[i] for i in range(COLUMNS)]
        mine = jnp.where(core == 1, swap_low(me), me)
        row = pl.multiple_of(step * HALF, HALF)
        for i in range(0, COLUMNS, 2):
            place = (facet_row * (COLUMNS // 2) + i // 2) ^ (mine >> 1)
            odd = (mine & 1) == 1
            keep_ref[place, pl.ds(row, HALF), :] = jnp.where(odd, tiles[i + 1], tiles[i])
            send_ref[place, pl.ds(row, HALF), :] = jnp.where(odd, tiles[i], tiles[i + 1])

    @pl.when(jnp.max(own_ref[step, 2 * channels + 40 : 2 * channels + 48]) > 0.0)
    def _():
        build(0)
        product = None
        for c in range(0, 2 * channels, 2):
            if c == channels // 2:
                build(1)
            for i in range(2):
                add_rows(c // channels, c % channels + i)
            right = jnp.concatenate([right_ref[c, 0:256], right_ref[c + 1, 0:256]], axis=1)
            left = jnp.concatenate([left_ref[c, 0:256], left_ref[c + 1, 0:256]], axis=1)
            term = dot(right, left, 1)
            product = term if product is None else product + term
        store(finish(product))


def grid_blocks(own, other):
    facet_total = lax.axis_size("facet")
    half_blocks = own.shape[0]
    channels, lanes = other.shape[3:]
    out = jax.ShapeDtypeStruct((facet_total // 2, half_blocks * HALF, 128), jnp.float32)
    vmem = pl.BlockSpec(memory_space=pltpu.VMEM)
    return pl.pallas_call(
        grid_kernel,
        grid=(facet_total // COLUMNS, half_blocks),
        in_specs=[vmem, vmem],
        out_specs=[vmem, vmem],
        scratch_shapes=[
            pltpu.VMEM((2, COLUMNS + 4, channels + 8, lanes), jnp.float32),
            pltpu.VMEM((2, BASE * channels, lanes), jnp.float32),
            pltpu.VMEM((2 * channels, 256 + PAD, lanes), jnp.bfloat16),
            pltpu.VMEM((2 * channels, 256 + PAD, lanes), jnp.bfloat16),
        ],
        out_shape=[out, out],
        compiler_params=pltpu.CompilerParams(vmem_limit_bytes=40 * 1024 * 1024),
        name="grid_blocks",
    )(own, other)


def image_tables(band_total, scale):
    offsets = np.arange(SUB) - HALF
    pixels = np.arange(G) - G // 2
    taper = 1.0 - 0.8 * (offsets / HALF) ** 2
    spread = np.exp(2j * np.pi * np.outer(pixels, offsets) / G)
    table = spread @ np.exp(-2j * np.pi * np.outer(offsets, offsets) / SUB) * taper
    share = G // band_total
    first = np.zeros((2, band_total, 4, share, 4, SUB))
    for sign in range(2):
        for band in range(band_total):
            wave = table[band * share : (band + 1) * share, :: 1 if sign == 0 else -1]
            for odd in range(2):
                first[sign, band, 2 * odd, :, odd] = wave.real
                first[sign, band, 2 * odd + 1, :, odd] = wave.imag
                first[sign, band, 2 * odd, :, 2 + odd] = -wave.imag
                first[sign, band, 2 * odd + 1, :, 2 + odd] = wave.real
    first = first.reshape(2 * band_total, 1, 4 * share, 4 * SUB).astype(np.float32)
    high = first.astype(ml_dtypes.bfloat16)
    low = (first - high.astype(np.float32)).astype(ml_dtypes.bfloat16)
    upper, lower = table.T[HALF:], table.T[HALF - 1 :: -1]
    second = np.stack([(upper + lower).real, (upper + lower).imag, (upper - lower).real, (upper - lower).imag]) * scale
    return np.concatenate([high, low], axis=1), second.astype(np.float32)


def two_parts(value):
    high = value.astype(jnp.bfloat16)
    return high, (value - high.astype(jnp.float32)).astype(jnp.bfloat16)


def down_kernel(owners_ref, corners_ref, assign_ref, counts_ref, after_ref, down_ref, weight_ref):
    band = lax.axis_index("freq")
    blocks = corners_ref.shape[2]
    share, rows = down_ref.shape[1:]
    for item in range(2 * blocks):
        weight_ref[assign_ref[0, item]] = (item < counts_ref[0]).astype(jnp.int32)
    group = lax.broadcasted_iota(jnp.int32, (1, rows), 1) // HALF
    corner, weight = jnp.zeros((1, rows), jnp.int32), jnp.zeros((1, rows), jnp.int32)
    for b in range(2 * blocks):
        corner = jnp.where(group == b, corners_ref[0, owners_ref[b // blocks], b % blocks] - centre_shift, corner)
        weight = jnp.where(group == b, weight_ref[b], weight)
    down = lax.broadcasted_iota(jnp.int32, (share, 1), 0) - G // 2 + band * share
    wave = cos_sin(((down * corner) & (G - 1)).astype(jnp.float32) * (1.0 / G))
    for part in range(2):
        down_ref[part] = wave[part] * weight.astype(jnp.float32)


def across_kernel(
    owners_ref, corners_ref, second_ref, tables_ref, after_ref, across_ref, first_ref, turn_ref, first_sem
):
    left_half = (lax.axis_index("facet") % COLUMNS < COLUMNS // 2).astype(jnp.int32)
    index = left_half * lax.axis_size("freq") + lax.axis_index("freq")
    copy = pltpu.make_async_copy(tables_ref.at[index], first_ref, first_sem)
    copy.start()
    blocks = corners_ref.shape[2]
    rows = 2 * blocks * HALF
    pixels = across_ref.shape[2]
    across = lax.broadcasted_iota(jnp.int32, (1, pixels), 1) - pixels // 2
    for b in range(2 * blocks):
        turn_ref[b : b + 1] = across * (corners_ref[1, owners_ref[b // blocks], b % blocks] - centre_shift)
    wave = cos_sin((turn_ref[...] & (G - 1)).astype(jnp.float32) * (1.0 / G))
    full = rows - rows % 128
    for b in range(2 * blocks):
        for odd in range(2):
            real, imag = times((second_ref[2 * odd], second_ref[2 * odd + 1]), (wave[0][b : b + 1], wave[1][b : b + 1]))
            for k, value in enumerate((real, -imag)):
                kind = 2 * odd + k
                at = kind * full + HALF * b if HALF * b < full else 4 * full + kind * (rows - full) + HALF * b - full
                high, low = two_parts(value)
                across_ref[0, at : at + HALF] = high
                across_ref[1, at : at + HALF] = low
    copy.wait()


def image_kernel(own_ref, other_ref, down_ref, across_ref, first_ref, out_ref):
    core = lax.axis_index("freq") & 1
    share = out_ref.shape[1]
    mine = core == 0
    pieces = []
    for s in range(2):
        own, other = own_ref[s], other_ref[s]
        pieces += [jnp.where(mine, own, other), jnp.where(mine, other, own)]
    high, low = two_parts(jnp.concatenate(pieces, axis=0))
    table_high, table_low = first_ref[0], first_ref[1]
    half = dot(table_high, high, 1) + (dot(table_high, low, 1) + dot(table_low, high, 1))
    wave = (down_ref[0], down_ref[1])
    kinds = []
    for odd in range(2):
        at = 2 * odd * share
        kinds += list(times((half[at : at + share], half[at + share : at + 2 * share]), wave))
    rows = half.shape[1]
    full = rows - rows % 128
    pieces = [kind[:, :full] for kind in kinds] + ([kind[:, full:] for kind in kinds] if full < rows else [])
    high, low = two_parts(jnp.concatenate(pieces, axis=1))
    both = dot(jnp.concatenate([high, low], axis=0), across_ref[0], 0)
    out_ref[0] = both[:share] + (both[share:] + dot(high, across_ref[1], 0))


def down_of(owners, corners, assign, counts, after):
    share = G // lax.axis_size("freq")
    total = 2 * corners.shape[2]
    smem = pl.BlockSpec(memory_space=pltpu.SMEM)
    return pl.pallas_call(
        down_kernel,
        in_specs=[smem, smem, smem, smem, pl.BlockSpec(memory_space=pl.ANY)],
        out_specs=pl.BlockSpec(memory_space=pltpu.VMEM),
        out_shape=jax.ShapeDtypeStruct((2, share, total * HALF), jnp.float32),
        scratch_shapes=[pltpu.SMEM((total,), jnp.int32)],
        compiler_params=pltpu.CompilerParams(vmem_limit_bytes=32 * 1024 * 1024),
        cost_estimate=pl.CostEstimate(flops=10**7, bytes_accessed=10**6, transcendentals=0),
        name="image_down",
    )(owners, corners, assign, counts, after)


def across_of(owners, corners, second, first, after):
    total = 2 * corners.shape[2]
    smem, vmem = pl.BlockSpec(memory_space=pltpu.SMEM), pl.BlockSpec(memory_space=pltpu.VMEM)
    return pl.pallas_call(
        across_kernel,
        in_specs=[smem, smem, vmem] + [pl.BlockSpec(memory_space=pl.ANY)] * 2,
        out_specs=[vmem, vmem],
        out_shape=[
            jax.ShapeDtypeStruct((2, 4 * total * HALF, G), jnp.bfloat16),
            jax.ShapeDtypeStruct(first.shape[1:], first.dtype),
        ],
        scratch_shapes=[pltpu.VMEM((total, G), jnp.int32), pltpu.SemaphoreType.DMA(())],
        compiler_params=pltpu.CompilerParams(vmem_limit_bytes=32 * 1024 * 1024),
        cost_estimate=pl.CostEstimate(flops=10**8, bytes_accessed=6 * 10**6, transcendentals=0),
        name="image_across",
    )(owners, corners, second, first, after)


def image_blocks(down, across, first, own, other):
    share, pixels = down.shape[1], across.shape[2]
    return pl.pallas_call(
        image_kernel,
        in_specs=[pl.BlockSpec(memory_space=pltpu.VMEM)] * 5,
        out_specs=pl.BlockSpec(memory_space=pltpu.VMEM),
        out_shape=jax.ShapeDtypeStruct((1, share, pixels), jnp.float32),
        compiler_params=pltpu.CompilerParams(vmem_limit_bytes=40 * 1024 * 1024),
        name="image_blocks",
    )(own, other, down, across, first)


def swap(value, partner):
    facet_total, band_total = lax.axis_size("facet"), lax.axis_size("freq")
    pairs = []
    for f in range(facet_total):
        for q in range(band_total):
            to_f, to_q = partner(f, q)
            pairs.append((f * band_total + q, to_f * band_total + to_q))
    return lax.ppermute(value, ("facet", "freq"), pairs)


def on_device(visibilities, coords, corners, owners, assign, counts):
    facet_total, band_total = lax.axis_size("facet"), lax.axis_size("freq")
    facet_index, band_index = lax.axis_index("facet"), lax.axis_index("freq")
    channel_total = visibilities.shape[3] * band_total
    scale = 1.0 / (SUB * SUB * math.sqrt(2 * corners.shape[2] * visibilities.shape[4] * channel_total))
    first, second = (jnp.asarray(x) for x in image_tables(band_total, scale))
    other = swap(visibilities, lambda f, q: (f, q ^ 1))
    own = gather(owners, corners, coords, visibilities)
    kept, sent = grid_blocks(own, other)
    half_rows = kept.shape[1]
    kept, sent = kept[None], sent[None]
    for k in range(facet_total.bit_length() - 1):
        even, odd = (k, k ^ 1) if k < 2 else (k, k)
        if k > 0:
            parts = held.reshape(2, -1, 2, half_rows, 128)
            kept, sent = parts[:, :, 0], parts[:, :, 1]
        tables = ()
        if k == 0:
            tables = down_of(owners, corners, assign, counts, sent)
        if k == 1:
            tables = across_of(owners, corners, second, first, sent)
        came = swap(sent, lambda f, q: (f ^ (1 << (odd if q & 1 else even)), q))
        came, tables = lax.optimization_barrier((came, tables))
        if k == 0:
            down = tables
        if k == 1:
            across, first = tables
        bit = jnp.where(band_index & 1 == 1, odd, even)
        across_bit = ((owners ^ facet_index) >> bit & 1) == 1
        held = jnp.where(across_bit[:, None, None, None], came, kept)
    held = held.reshape(2, half_rows, 128)
    for k in range(1, band_total.bit_length() - 1):
        held = held + swap(held, lambda f, q: (f, q ^ (1 << k)))
    other = swap(held, lambda f, q: (f, q ^ 1))
    return image_blocks(down, across, first, held, other)


def solution(mesh):
    placed = (
        P("facet", None, None, "freq", None),
        P("facet", None, None, None),
        P(),
        P(),
        P("facet", None),
        P("facet"),
    )
    return jax.shard_map(
        on_device, mesh=mesh, in_specs=placed, out_specs=P("facet", "freq", None), check_vma=False
    )
```

```python
import math

import jax
import jax.numpy as jnp
import ml_dtypes
import numpy as np
from jax import lax
from jax.experimental import pallas as pl
from jax.experimental.pallas import tpu as pltpu
from jax.sharding import PartitionSpec as P

SUB = 32
G = 512
HALF = SUB // 2
COLUMNS = 8
BASE = 72
PAD = 16

two_pi = 2.0 * math.pi
field_width = 0.02
band_spread = 0.02
centre_shift = G // 2 - SUB // 2

SIN_POLY = (6.2831853, -41.34170041, 81.6051314, -76.70301553, 42.02592778, -14.89984801, 3.23813768)
COS_POLY = (0.99999999, -19.7392045, 64.9391175, -85.45013994, 60.16763282, -25.96760244, 6.52865863)


def poly(square, coefficients):
    total = jnp.full_like(square, coefficients[-1])
    for coefficient in coefficients[-2::-1]:
        total = total * square + coefficient
    return total


def cos_sin(turns):
    rest = turns - jnp.round(turns)
    square = rest * rest
    return poly(square, COS_POLY), rest * poly(square, SIN_POLY)


def times(a, b):
    return a[0] * b[0] - a[1] * b[1], a[0] * b[1] + a[1] * b[0]


def dot(a, b, over):
    return lax.dot_general(a, b, (((1,), (over,)), ((), ())), preferred_element_type=jnp.float32)


def swap_low(value):
    return (value & ~3) | ((value & 1) << 1) | ((value >> 1) & 1)


def gather_kernel(
    owners_hbm, corners_hbm, coords_hbm, vis_hbm, out_ref, owners_ref, corners_ref, coords_ref, sems
):
    me = lax.axis_index("facet")
    half_blocks = out_ref.shape[0]
    first = (lax.axis_index("freq") & 1) * half_blocks
    rows, lanes = vis_hbm.shape[1:]
    ends = (
        (vis_hbm.at[pl.ds(first, half_blocks)], out_ref.at[:, pl.ds(0, rows)]),
        (owners_hbm, owners_ref),
        (corners_hbm, corners_ref),
        (coords_hbm.at[pl.ds(first, half_blocks)], coords_ref),
    )
    copies = [pltpu.make_async_copy(source, target, sems.at[k]) for k, (source, target) in enumerate(ends)]
    for copy in copies:
        copy.start()
    for copy in copies[1:]:
        copy.wait()
    active = jnp.logical_or(owners_ref[0] == me, owners_ref[1] == me).astype(jnp.float32)
    for b in range(half_blocks):
        shifts = [(centre_shift - corners_ref[i, me, first + b]).astype(jnp.float32) for i in range(2)]
        for i, value in enumerate([coords_ref[b, i] for i in range(3)] + shifts + [active]):
            out_ref[b, rows + 8 * i : rows + 8 * i + 8] = jnp.broadcast_to(value, (8, lanes))
    copies[0].wait()


def gather(owners, corners, coords, visibilities):
    _, blocks, _, channels, lanes = visibilities.shape
    rows = 2 * channels
    return pl.pallas_call(
        gather_kernel,
        in_specs=[pl.BlockSpec(memory_space=pltpu.HBM)] * 4,
        out_specs=pl.BlockSpec(memory_space=pltpu.VMEM),
        out_shape=jax.ShapeDtypeStruct((blocks // 2, rows + 48, lanes), jnp.float32),
        scratch_shapes=[
            pltpu.SMEM(owners.shape, jnp.int32),
            pltpu.SMEM(corners.shape, jnp.int32),
            pltpu.VMEM((blocks // 2, 3, 1, lanes), jnp.float32),
            pltpu.SemaphoreType.DMA((4,)),
        ],
        compiler_params=pltpu.CompilerParams(vmem_limit_bytes=60 * 1024 * 1024),
        name="gather_blocks",
    )(owners, corners, coords.reshape(blocks, 3, 1, lanes), visibilities.reshape(blocks, rows, lanes))


def grid_kernel(own_ref, other_ref, keep_ref, send_ref, z_ref, base_ref, left_ref, right_ref):
    me = lax.axis_index("facet")
    band = lax.axis_index("freq")
    band_total = lax.axis_size("freq")
    facet_rows = lax.axis_size("facet") // COLUMNS
    core = band & 1
    facet_row = pl.program_id(0)
    step = pl.program_id(1)
    half_blocks = own_ref.shape[0]
    channels, lanes = other_ref.shape[3], other_ref.shape[4]
    block = core * half_blocks + step

    def build(k):
        first_channel = (band ^ k) * channels
        channel = (first_channel + lax.broadcasted_iota(jnp.int32, (channels, lanes), 0)).astype(jnp.float32)
        ratio = 1.0 + band_spread * channel / (channels * band_total)
        u, v, w, shift_u, shift_v = (own_ref[step, 2 * channels + 8 * i : 2 * channels + 8 * i + 1] for i in range(5))
        u_cells, v_cells, w_waves = u * ratio, v * ratio, w * ratio
        delta_u = u_cells + shift_u
        delta_v = v_cells + shift_v
        half_turn = 0.5 * shift_u - jnp.round(0.5 * shift_u)
        row_pos = facet_row.astype(jnp.float32) - (facet_rows - 1) / 2.0
        row_vec = jnp.full((8, lanes), row_pos, jnp.float32)
        common = v_cells * row_pos - (delta_u + delta_v) * (0.5 / SUB) + half_turn
        if k == 0:
            vis = (own_ref[step, 0:channels], own_ref[step, channels : 2 * channels])
        else:
            vis = (other_ref[0, block, 0], other_ref[0, block, 1])
        for g in range(COLUMNS // 2):
            radius = field_width * field_width * ((g + 0.5) ** 2 + row_vec * row_vec)
            w_shift = (-radius / (1.0 + jnp.sqrt(1.0 - radius)))[0:1]
            turned = times(vis, cos_sin(common + w_waves * w_shift))
            z_ref[k, 2 * g, 0:channels] = turned[0]
            z_ref[k, 2 * g + 1, 0:channels] = turned[1]
        for axis, delta in enumerate((delta_u, delta_v)):
            wave = cos_sin(delta * (0.5 / SUB))
            turn = times(wave, wave)
            for j in range(16):
                base_ref[k, pl.ds(32 * axis + j, channels, stride=BASE), :] = wave[0]
                base_ref[k, pl.ds(32 * axis + 16 + j, channels, stride=BASE), :] = wave[1]
                if j == 0:
                    last, wave = wave, times(wave, turn)
                    twice = 2.0 * turn[0]
                elif j < 15:
                    last, wave = wave, tuple(twice * wave[part] - last[part] for part in range(2))
            if axis == 1:
                break
            for _ in range(3):
                turn = times(turn, turn)
            z_ref[k, COLUMNS, 0:channels] = 2.0 * turn[0]

    def add_rows(k, c):
        def row_of(i):
            return z_ref[k, i, c : c + 1]

        def base_of(i):
            return base_ref[k, BASE * c + 8 * i : BASE * c + 8 * i + 8, :]

        at = k * channels + c
        twice = row_of(COLUMNS)
        wave = (base_of(0), base_of(2))
        after = (base_of(1), base_of(3))
        for i in range(COLUMNS):
            for part in range(2):
                left_ref[at, 128 * part + 16 * i : 128 * part + 16 * i + 16] = jnp.concatenate(
                    [wave[part], after[part]], axis=0
                ).astype(jnp.bfloat16)
            if i < COLUMNS - 1:
                wave = tuple(twice * after[part] - wave[part] for part in range(2))
                after = tuple(twice * wave[part] - after[part] for part in range(2))
        both = tuple(base_ref[k, BASE * c + 32 + 16 * i : BASE * c + 48 + 16 * i, :] for i in range(2))
        for g in range(COLUMNS // 2):
            for part in range(2):
                turned = row_of(2 * g + part)
                for kind in range(2):
                    row = 64 * g + 32 * part + 16 * kind
                    right_ref[at, row : row + 16] = (turned * both[kind]).astype(jnp.bfloat16)

    def finish(product):
        group = lax.broadcasted_iota(jnp.int32, (HALF, 128), 1) // SUB
        tiles = [None] * COLUMNS
        for sign in (1, -1):
            for g in range(COLUMNS // 2):
                part = [product[64 * g + 16 * k : 64 * g + 16 * k + 16] for k in range(4)]
                (rcc, rcs), (rsc, rss), (icc, ics), (isc, iss) = [(x[:, :128], x[:, 128:]) for x in part]
                kinds = (rcc - sign * ics, -(sign * rss + isc), icc + sign * rcs, rsc - sign * iss)
                tile = None
                for t in range(4):
                    moved = kinds[t] if t == g else pltpu.roll(kinds[t], SUB * ((t - g) % 4), 1)
                    tile = moved if tile is None else jnp.where(group == t, moved, tile)
                tiles[COLUMNS // 2 + g if sign == 1 else COLUMNS // 2 - 1 - g] = tile
        return tiles

    def store(tiles):
        tiles = [jnp.where(core == 1, tiles[swap_low(i)], tiles[i]) if swap_low(i) != i else tiles[i] for i in range(COLUMNS)]
        mine = jnp.where(core == 1, swap_low(me), me)
        row = pl.multiple_of(step * HALF, HALF)
        for i in range(0, COLUMNS, 2):
            place = (facet_row * (COLUMNS // 2) + i // 2) ^ (mine >> 1)
            odd = (mine & 1) == 1
            keep_ref[place, pl.ds(row, HALF), :] = jnp.where(odd, tiles[i + 1], tiles[i])
            send_ref[place, pl.ds(row, HALF), :] = jnp.where(odd, tiles[i], tiles[i + 1])

    @pl.when(jnp.max(own_ref[step, 2 * channels + 40 : 2 * channels + 48]) > 0.0)
    def _():
        build(0)
        product = None
        for c in range(0, 2 * channels, 2):
            if c == channels // 2:
                build(1)
            for i in range(2):
                add_rows(c // channels, c % channels + i)
            right = jnp.concatenate([right_ref[c, 0:256], right_ref[c + 1, 0:256]], axis=1)
            left = jnp.concatenate([left_ref[c, 0:256], left_ref[c + 1, 0:256]], axis=1)
            term = dot(right, left, 1)
            product = term if product is None else product + term
        store(finish(product))


def grid_blocks(own, other):
    facet_total = lax.axis_size("facet")
    half_blocks = own.shape[0]
    channels, lanes = other.shape[3:]
    out = jax.ShapeDtypeStruct((facet_total // 2, half_blocks * HALF, 128), jnp.float32)
    vmem = pl.BlockSpec(memory_space=pltpu.VMEM)
    return pl.pallas_call(
        grid_kernel,
        grid=(facet_total // COLUMNS, half_blocks),
        in_specs=[vmem, vmem],
        out_specs=[vmem, vmem],
        scratch_shapes=[
            pltpu.VMEM((2, COLUMNS + 4, channels + 8, lanes), jnp.float32),
            pltpu.VMEM((2, BASE * channels, lanes), jnp.float32),
            pltpu.VMEM((2 * channels, 256 + PAD, lanes), jnp.bfloat16),
            pltpu.VMEM((2 * channels, 256 + PAD, lanes), jnp.bfloat16),
        ],
        out_shape=[out, out],
        compiler_params=pltpu.CompilerParams(vmem_limit_bytes=40 * 1024 * 1024),
        name="grid_blocks",
    )(own, other)


def image_tables(band_total, scale):
    offsets = np.arange(SUB) - HALF
    pixels = np.arange(G) - G // 2
    taper = 1.0 - 0.8 * (offsets / HALF) ** 2
    spread = np.exp(2j * np.pi * np.outer(pixels, offsets) / G)
    table = spread @ np.exp(-2j * np.pi * np.outer(offsets, offsets) / SUB) * taper
    share = G // band_total
    first = np.zeros((2, band_total, 4, share, 4, SUB))
    for sign in range(2):
        for band in range(band_total):
            wave = table[band * share : (band + 1) * share, :: 1 if sign == 0 else -1]
            for odd in range(2):
                first[sign, band, 2 * odd, :, odd] = wave.real
                first[sign, band, 2 * odd + 1, :, odd] = wave.imag
                first[sign, band, 2 * odd, :, 2 + odd] = -wave.imag
                first[sign, band, 2 * odd + 1, :, 2 + odd] = wave.real
    first = first.reshape(2 * band_total, 1, 4 * share, 4 * SUB).astype(np.float32)
    high = first.astype(ml_dtypes.bfloat16)
    low = (first - high.astype(np.float32)).astype(ml_dtypes.bfloat16)
    upper, lower = table.T[HALF:], table.T[HALF - 1 :: -1]
    second = np.stack([(upper + lower).real, (upper + lower).imag, (upper - lower).real, (upper - lower).imag]) * scale
    return np.concatenate([high, low], axis=1), second.astype(np.float32)


def two_parts(value):
    high = value.astype(jnp.bfloat16)
    return high, (value - high.astype(jnp.float32)).astype(jnp.bfloat16)


def down_kernel(owners_ref, corners_ref, assign_ref, counts_ref, after_ref, down_ref, weight_ref):
    band = lax.axis_index("freq")
    blocks = corners_ref.shape[2]
    share, rows = down_ref.shape[1:]
    for item in range(2 * blocks):
        weight_ref[assign_ref[0, item]] = (item < counts_ref[0]).astype(jnp.int32)
    group = lax.broadcasted_iota(jnp.int32, (1, rows), 1) // HALF
    corner, weight = jnp.zeros((1, rows), jnp.int32), jnp.zeros((1, rows), jnp.int32)
    for b in range(2 * blocks):
        corner = jnp.where(group == b, corners_ref[0, owners_ref[b // blocks], b % blocks] - centre_shift, corner)
        weight = jnp.where(group == b, weight_ref[b], weight)
    down = lax.broadcasted_iota(jnp.int32, (share, 1), 0) - G // 2 + band * share
    wave = cos_sin(((down * corner) & (G - 1)).astype(jnp.float32) * (1.0 / G))
    for part in range(2):
        down_ref[part] = wave[part] * weight.astype(jnp.float32)


def across_kernel(
    owners_ref, corners_ref, second_ref, tables_ref, after_ref, across_ref, first_ref, turn_ref, first_sem
):
    left_half = (lax.axis_index("facet") % COLUMNS < COLUMNS // 2).astype(jnp.int32)
    index = left_half * lax.axis_size("freq") + lax.axis_index("freq")
    copy = pltpu.make_async_copy(tables_ref.at[index], first_ref, first_sem)
    copy.start()
    blocks = corners_ref.shape[2]
    rows = 2 * blocks * HALF
    pixels = across_ref.shape[2]
    across = lax.broadcasted_iota(jnp.int32, (1, pixels), 1) - pixels // 2
    for b in range(2 * blocks):
        turn_ref[b : b + 1] = across * (corners_ref[1, owners_ref[b // blocks], b % blocks] - centre_shift)
    wave = cos_sin((turn_ref[...] & (G - 1)).astype(jnp.float32) * (1.0 / G))
    full = rows - rows % 128
    for b in range(2 * blocks):
        for odd in range(2):
            real, imag = times((second_ref[2 * odd], second_ref[2 * odd + 1]), (wave[0][b : b + 1], wave[1][b : b + 1]))
            for k, value in enumerate((real, -imag)):
                kind = 2 * odd + k
                at = kind * full + HALF * b if HALF * b < full else 4 * full + kind * (rows - full) + HALF * b - full
                high, low = two_parts(value)
                across_ref[0, at : at + HALF] = high
                across_ref[1, at : at + HALF] = low
    copy.wait()


def image_kernel(own_ref, other_ref, down_ref, across_ref, first_ref, out_ref):
    core = lax.axis_index("freq") & 1
    share = out_ref.shape[1]
    mine = core == 0
    pieces = []
    for s in range(2):
        own, other = own_ref[s], other_ref[s]
        pieces += [jnp.where(mine, own, other), jnp.where(mine, other, own)]
    high, low = two_parts(jnp.concatenate(pieces, axis=0))
    table_high, table_low = first_ref[0], first_ref[1]
    half = dot(table_high, high, 1) + (dot(table_high, low, 1) + dot(table_low, high, 1))
    wave = (down_ref[0], down_ref[1])
    kinds = []
    for odd in range(2):
        at = 2 * odd * share
        kinds += list(times((half[at : at + share], half[at + share : at + 2 * share]), wave))
    rows = half.shape[1]
    full = rows - rows % 128
    pieces = [kind[:, :full] for kind in kinds] + ([kind[:, full:] for kind in kinds] if full < rows else [])
    high, low = two_parts(jnp.concatenate(pieces, axis=1))
    both = dot(jnp.concatenate([high, low], axis=0), across_ref[0], 0)
    out_ref[0] = both[:share] + (both[share:] + dot(high, across_ref[1], 0))


def down_of(owners, corners, assign, counts, after):
    share = G // lax.axis_size("freq")
    total = 2 * corners.shape[2]
    smem = pl.BlockSpec(memory_space=pltpu.SMEM)
    return pl.pallas_call(
        down_kernel,
        in_specs=[smem, smem, smem, smem, pl.BlockSpec(memory_space=pl.ANY)],
        out_specs=pl.BlockSpec(memory_space=pltpu.VMEM),
        out_shape=jax.ShapeDtypeStruct((2, share, total * HALF), jnp.float32),
        scratch_shapes=[pltpu.SMEM((total,), jnp.int32)],
        compiler_params=pltpu.CompilerParams(vmem_limit_bytes=32 * 1024 * 1024),
        cost_estimate=pl.CostEstimate(flops=10**7, bytes_accessed=10**6, transcendentals=0),
        name="image_down",
    )(owners, corners, assign, counts, after)


def across_of(owners, corners, second, first, after):
    total = 2 * corners.shape[2]
    smem, vmem = pl.BlockSpec(memory_space=pltpu.SMEM), pl.BlockSpec(memory_space=pltpu.VMEM)
    return pl.pallas_call(
        across_kernel,
        in_specs=[smem, smem, vmem] + [pl.BlockSpec(memory_space=pl.ANY)] * 2,
        out_specs=[vmem, vmem],
        out_shape=[
            jax.ShapeDtypeStruct((2, 4 * total * HALF, G), jnp.bfloat16),
            jax.ShapeDtypeStruct(first.shape[1:], first.dtype),
        ],
        scratch_shapes=[pltpu.VMEM((total, G), jnp.int32), pltpu.SemaphoreType.DMA(())],
        compiler_params=pltpu.CompilerParams(vmem_limit_bytes=32 * 1024 * 1024),
        cost_estimate=pl.CostEstimate(flops=10**8, bytes_accessed=6 * 10**6, transcendentals=0),
        name="image_across",
    )(owners, corners, second, first, after)


def image_blocks(down, across, first, own, other):
    share, pixels = down.shape[1], across.shape[2]
    return pl.pallas_call(
        image_kernel,
        in_specs=[pl.BlockSpec(memory_space=pltpu.VMEM)] * 5,
        out_specs=pl.BlockSpec(memory_space=pltpu.VMEM),
        out_shape=jax.ShapeDtypeStruct((1, share, pixels), jnp.float32),
        compiler_params=pltpu.CompilerParams(vmem_limit_bytes=40 * 1024 * 1024),
        name="image_blocks",
    )(own, other, down, across, first)


def swap(value, partner):
    facet_total, band_total = lax.axis_size("facet"), lax.axis_size("freq")
    pairs = []
    for f in range(facet_total):
        for q in range(band_total):
            to_f, to_q = partner(f, q)
            pairs.append((f * band_total + q, to_f * band_total + to_q))
    return lax.ppermute(value, ("facet", "freq"), pairs)


def on_device(visibilities, coords, corners, owners, assign, counts):
    facet_total, band_total = lax.axis_size("facet"), lax.axis_size("freq")
    facet_index, band_index = lax.axis_index("facet"), lax.axis_index("freq")
    channel_total = visibilities.shape[3] * band_total
    scale = 1.0 / (SUB * SUB * math.sqrt(2 * corners.shape[2] * visibilities.shape[4] * channel_total))
    first, second = (jnp.asarray(x) for x in image_tables(band_total, scale))
    other = swap(visibilities, lambda f, q: (f, q ^ 1))
    own = gather(owners, corners, coords, visibilities)
    kept, sent = grid_blocks(own, other)
    half_rows = kept.shape[1]
    kept, sent = kept[None], sent[None]
    for k in range(facet_total.bit_length() - 1):
        even, odd = (k, k ^ 1) if k < 2 else (k, k)
        if k > 0:
            parts = held.reshape(2, -1, 2, half_rows, 128)
            kept, sent = parts[:, :, 0], parts[:, :, 1]
        tables = ()
        if k == 0:
            tables = down_of(owners, corners, assign, counts, sent)
        if k == 1:
            tables = across_of(owners, corners, second, first, sent)
        came = swap(sent, lambda f, q: (f ^ (1 << (odd if q & 1 else even)), q))
        came, tables = lax.optimization_barrier((came, tables))
        if k == 0:
            down = tables
        if k == 1:
            across, first = tables
        bit = jnp.where(band_index & 1 == 1, odd, even)
        across_bit = ((owners ^ facet_index) >> bit & 1) == 1
        held = jnp.where(across_bit[:, None, None, None], came, kept)
    held = held.reshape(2, half_rows, 128)
    for k in range(1, band_total.bit_length() - 1):
        held = held + swap(held, lambda f, q: (f, q ^ (1 << k)))
    other = swap(held, lambda f, q: (f, q ^ 1))
    return image_blocks(down, across, first, held, other)


def solution(mesh):
    placed = (
        P("facet", None, None, "freq", None),
        P("facet", None, None, None),
        P(),
        P(),
        P("facet", None),
        P("facet"),
    )
    return jax.shard_map(
        on_device, mesh=mesh, in_specs=placed, out_specs=P("facet", "freq", None), check_vma=False
    )
```
